256 devices in a mesh: blk: 256 (over z, x, y, core).
Axes of the slice: x: 4, y: 4, z: 8, core: 2. Of those that a mesh axis runs over, the one named last changes fastest.
Arguments:
- points: float32 [11, 65536], P(None, 'blk'), may hold values from -6 to 6
- lengthscales: float32 [11], replicated, may hold values from 1.5 to 6
- noise: float32 [1], replicated, may hold values from 0.5 to 2
- solution: float32 [16, 65536], P(None, 'blk'), may hold values from -6 to 6
- residual: float32 [16, 65536], P(None, 'blk'), may hold values from -6 to 6
- direction: float32 [16, 65536], P(None, 'blk'), may hold values from -6 to 6
Outputs:
- solution_next: float32 [16, 65536], P(None, 'blk')
- residual_next: float32 [16, 65536], P(None, 'blk')
- direction_next: float32 [16, 65536], P(None, 'blk')
The draws below stay inside these ranges and needn't reach their ends.
All inputs are finite; a program needn't handle non-finite values.
Results may differ from the reference program's by a relative error of at most 0.0003.
Values sent between devices are 32-bit elements; how exact they have to be, the bound alone decides.
A program may use at most 192 MiB of HBM per device.

```python
import math
import jax
import jax.numpy as jnp
from jax import lax

FEAT = 11
RHS = 16
NPTS = 65536


def shard_levels(rng, shape, cuts, low, largest):
    loudness, own = 1.0, jax.random.fold_in(rng, 6)
    for position, blocks in cuts:
        steps = jnp.exp(jax.random.uniform(jax.random.fold_in(own, position), (blocks,), jnp.float32, low / len(cuts), largest / len(cuts)))
        loudness = loudness * jnp.repeat(steps, shape[position] // blocks).reshape([-1 if axis == position else 1 for axis in range(len(shape))])
    return loudness


def centred(stream_key, shape, scale, limit, split=(), kind=jnp.bfloat16):
    values = scale * jax.random.normal(stream_key, shape, jnp.float32)
    if split:
        values = values * shard_levels(stream_key, shape, split, -0.22, 0.18)
    return jnp.clip(values, -limit, limit).astype(kind)


def setup_inputs(seed: int = 0) -> dict:
    seeds = jax.random.split(jax.random.key(seed), 7)
    return {
        "points": centred(seeds[0], (FEAT, NPTS), 1.0, 6.0, ((1, 256),), jnp.float32),
        "lengthscales": jnp.clip(jnp.exp(jax.random.uniform(seeds[1], (FEAT,), jnp.float32, math.log(1.5), math.log(6.0))), 1.5, 6.0),
        "noise": jnp.clip(jax.random.uniform(seeds[2], (1,), jnp.float32, 0.5, 2.0), 0.5, 2.0),
        "solution": centred(seeds[3], (RHS, NPTS), 1.0, 6.0, ((1, 256),), jnp.float32),
        "residual": centred(seeds[4], (RHS, NPTS), 1.0, 6.0, ((1, 256),), jnp.float32),
        "direction": centred(seeds[5], (RHS, NPTS), 1.0, 6.0, ((1, 256),), jnp.float32),
    }


def matern(left, right, lengthscales):
    scaled_left = left / lengthscales[:, None]
    scaled_right = right / lengthscales[:, None]
    dist_sq = jnp.zeros((left.shape[1], right.shape[1]), jnp.float32)
    for feature in range(left.shape[0]):
        diff = scaled_left[feature][:, None] - scaled_right[feature][None, :]
        dist_sq = dist_sq + diff * diff
    scaled = jnp.sqrt(5.0 * dist_sq)
    return (1.0 + scaled + scaled * scaled / 3.0) * jnp.exp(-scaled)

def reference(points, lengthscales, noise, solution, residual, direction):
    rows = math.gcd(NPTS, 512)
    count = NPTS // rows
    blocks = points.reshape(FEAT, count, rows).transpose(1, 0, 2)

    def one_block(block):
        tile = matern(block, points, lengthscales)
        return lax.dot_general(direction, tile, (((1,), (1,)), ((), ())), precision=lax.Precision.HIGHEST, preferred_element_type=jnp.float32)
    parts = lax.map(one_block, blocks)
    image = parts.transpose(1, 0, 2).reshape(RHS, NPTS) + noise[0] * direction
    norm_now = lax.optimization_barrier(jnp.sum(residual * residual, axis=1))
    curv = lax.optimization_barrier(jnp.sum(direction * image, axis=1))
    alpha = norm_now / curv
    solution_next = solution + alpha[:, None] * direction
    residual_next = residual - alpha[:, None] * image
    norm_next = lax.optimization_barrier(jnp.sum(residual_next * residual_next, axis=1))
    direction_next = residual_next + (norm_next / norm_now)[:, None] * direction
    return (solution_next, residual_next, direction_next)
```

```python
import math

import jax
import jax.numpy as jnp
from jax import lax
from jax.experimental import pallas as pl
from jax.experimental.pallas import tpu as pltpu
from jax.sharding import PartitionSpec as P

MESH = pl.DeviceIdType.MESH
F32, BF16 = jnp.float32, jnp.bfloat16
SIDE = 16
SLOTS = 9
LN2 = math.log(2.0)
SCALE = math.sqrt(5.0) / LN2
CURVE = LN2 * LN2 / 3.0
BEND = 3.0 / LN2
LIFT = 3.0 / (LN2 * LN2)
LAST = (((1,), (1,)), ((), ()))


def three(value):
    high = value.astype(BF16).astype(F32)
    rest = value - high
    middle = rest.astype(BF16).astype(F32)
    return high, middle, (rest - middle).astype(BF16).astype(F32)


def two(value):
    high = value.astype(BF16)
    return high, (value - high.astype(F32)).astype(BF16)


def matern(square):
    square = jnp.maximum(square, 1e-30)
    root = square * lax.rsqrt(square)
    return (square + BEND * root + LIFT) * jnp.exp2(-root)


def kernel(
    scales_ref, noise_ref, points_ref, sol_ref, res_ref, dir_ref,
    sol_out, res_out, dir_out,
    rows, cols, left, right, dir_row, dir_col, acc_row, acc_col, square, high, low,
    out_row, out_col, in_row, in_col, stat_col, stat_row,
    row_send, row_recv, col_send, col_recv, rs_row_send, rs_row_recv, rs_col_send, rs_col_recv,
    sc_send, sc_recv, sr_send, sr_recv,
):
    me = lax.axis_index("blk")
    down = lax.rem(me // 2, SIDE)
    across = (me // (2 * SIDE)) * 2 + lax.rem(me, 2)

    def device(i, l):
        i, l = lax.rem(i, SIDE), lax.rem(l, SIDE)
        return ((l // 2) * (2 * SIDE) + i * 2 + lax.rem(l, 2),)

    def step_of(slot):
        odd = lax.rem(slot, 2)
        return odd * slot + (1 - odd) * (SIDE - slot)

    barrier = pltpu.get_barrier_semaphore()

    def greet(k, _):
        pl.semaphore_signal(barrier, inc=1, device_id=device(down + k, across), device_id_type=MESH)
        pl.semaphore_signal(barrier, inc=1, device_id=device(down, across + k), device_id_type=MESH)
        return 0

    lax.fori_loop(1, SIDE, greet, 0)

    line = lax.broadcasted_iota(jnp.int32, (SIDE, 256), 0)
    ratio = jnp.ones((SIDE, 256), F32)
    for f in range(11):
        ratio = jnp.where(line == f, scales_ref[f], ratio)
    cols[0, 0:16, :] = dir_ref[...]
    cols[0, 16:32, :] = jnp.zeros((16, 256), F32)
    cols[0, 16:27, :] = points_ref[...]
    feats = cols[0, 16:32, :] * (SCALE / ratio)
    norm = jnp.sum(feats * feats, axis=0, keepdims=True)
    block = jnp.where(line == 11, norm, jnp.where(line == 12, 1.0, feats))
    cols[0, 16:32, :] = block
    rows[0, 0:16, :] = dir_ref[...]
    rows[0, 16:32, :] = block

    pl.semaphore_wait(barrier, 2 * (SIDE - 1))

    def copy_row(s):
        return pltpu.make_async_remote_copy(
            src_ref=cols.at[0], dst_ref=rows.at[s], send_sem=row_send.at[s], recv_sem=row_recv.at[s],
            device_id=device(down, across + SIDE - step_of(s)), device_id_type=MESH)

    def copy_col(y):
        return pltpu.make_async_remote_copy(
            src_ref=cols.at[0], dst_ref=cols.at[y], send_sem=col_send.at[y], recv_sem=col_recv.at[y],
            device_id=device(down + SIDE - y, across), device_id_type=MESH)

    def go(make):
        def body(k, _):
            make(k).start()
            return 0
        return body

    def sent(make):
        def body(k, _):
            make(k).wait_send()
            return 0
        return body

    lax.fori_loop(1, SLOTS, go(copy_row), 0)
    lax.fori_loop(1, SIDE, go(copy_col), 0)

    acc_row[...] = jnp.zeros_like(acc_row)
    acc_col[...] = jnp.zeros_like(acc_col)
    square[...] = jnp.full_like(square, 1e6)
    high[...] = jnp.zeros_like(high)
    low[...] = jnp.zeros_like(low)

    def prep_row(s):
        dir_row[s] = jnp.concatenate(two(rows[s, 0:16, :]), axis=0)
        value = rows[s, 16:32, :]
        norm = jnp.sum(jnp.where(line == 11, value, 0.0), axis=0, keepdims=True)
        value = jnp.where(line == 11, 1.0, jnp.where(line == 12, norm, -2.0 * value))
        h, m, l = three(value)
        nil = jnp.zeros((SIDE, 256), F32)
        tall = jnp.concatenate([h, h, m, h, l, m, nil, nil], axis=0)
        left[s] = jnp.transpose(tall).astype(BF16)

    def prep_col(y):
        dir_col[y] = jnp.concatenate(two(cols[y, 0:16, :]), axis=0)
        h, m, l = three(cols[y, 16:32, :])
        nil = jnp.zeros((SIDE, 256), F32)
        right[y] = jnp.concatenate([h, m, h, l, h, m, nil, nil], axis=0).astype(BF16)

    prep_row(0)
    prep_col(0)

    def take_row(s, _):
        copy_row(s).wait_recv()
        prep_row(s)
        return 0

    def take_col(y, _):
        copy_col(y).wait_recv()
        prep_col(y)
        return 0

    lax.fori_loop(1, SLOTS, take_row, 0)
    lax.fori_loop(1, SIDE, take_col, 0)

    def places(t):
        g, pair = t // 8, lax.rem(t, 8)
        upper = pair // 4
        first = g * 4 + (1 - g) * upper * 8
        slots = [first, g * 4 + 1, g * 4 + 2, g * 4 + 3]
        ys = [pair * 2, pair * 2 + 1]
        ys0 = [y - (1 - g) * upper * 8 for y in ys]
        return g, slots, ys, ys0

    def dot(a, b):
        return jnp.dot(a, b, preferred_element_type=F32)

    def dot_t(a, b):
        return lax.dot_general(a, b, LAST, preferred_element_type=F32)

    def distance(s, y):
        return dot(left[s], right[y])

    def step(t, _):
        g, slots, ys, ys0 = places(jnp.maximum(t - 2, 0))
        _, slots_n, ys_n, ys0_n = places(jnp.minimum(t, 15))
        one_way = jnp.where((g == 0) & (ys0[0] == 0), 0.0, 1.0).astype(F32)
        side_sum = [None, None]
        for n in range(4):
            mine = None
            for j in range(2):
                k = n * 2 + j
                hi, lo = high[k], low[k]
                y = ys0[j] if n == 0 else ys[j]
                term = dot_t(dir_col[y], hi) + dot_t(dir_col[y], lo)
                mine = term if mine is None else mine + term
                drow = dir_row[slots[n]]
                term = dot(drow, hi) + dot(drow, lo)
                if n == 0:
                    if j == 0:
                        term = term * one_way
                    acc_col[y] += term
                else:
                    side_sum[j] = term if side_sum[j] is None else side_sum[j] + term
                hi, lo = two(matern(square[k]))
                high[k] = hi
                low[k] = lo
                y = ys0_n[j] if n == 0 else ys_n[j]
                square[k] = distance(slots_n[n], y)
            acc_row[slots[n]] += mine
        for j in range(2):
            acc_col[ys[j]] += side_sum[j]
        return 0

    lax.fori_loop(0, 18, step, 0)

    for s in (0, 8):
        hi, lo = two(matern(distance(s, 8)))
        acc_row[s] += dot_t(dir_col[8], hi) + dot_t(dir_col[8], lo)

    def give_row(s):
        return pltpu.make_async_remote_copy(
            src_ref=out_row.at[s], dst_ref=in_row.at[s], send_sem=rs_row_send.at[s], recv_sem=rs_row_recv.at[s],
            device_id=device(down, across + step_of(s)), device_id_type=MESH)

    def give_col(y):
        return pltpu.make_async_remote_copy(
            src_ref=out_col.at[y], dst_ref=in_col.at[y], send_sem=rs_col_send.at[y], recv_sem=rs_col_recv.at[y],
            device_id=device(down + y, across), device_id_type=MESH)

    def push_row(s, _):
        out_row[s] = acc_row[s, 0:16, :] + acc_row[s, 16:32, :]
        give_row(s).start()
        return 0

    def push_col(y, _):
        out_col[y] = acc_col[y, 0:16, :] + acc_col[y, 16:32, :]
        give_col(y).start()
        return 0

    lax.fori_loop(1, SLOTS, push_row, 0)
    lax.fori_loop(1, SIDE, push_col, 0)
    own = acc_row[0, 0:16, :] + acc_row[0, 16:32, :] + acc_col[0, 0:16, :] + acc_col[0, 16:32, :]

    def pull_row(s, total):
        give_row(s).wait_recv()
        return total + in_row[s]

    def pull_col(y, total):
        give_col(y).wait_recv()
        return total + in_col[y]

    own = lax.fori_loop(1, SLOTS, pull_row, own)
    own = lax.fori_loop(1, SIDE, pull_col, own)
    direction = dir_ref[...]
    residual = res_ref[...]
    image = CURVE * own + noise_ref[0] * direction

    def total(value):
        return jnp.sum(value, axis=1, keepdims=True)

    lane = lax.broadcasted_iota(jnp.int32, (16, 128), 1)
    stats = jnp.where(lane == 0, total(residual * residual), jnp.where(
        lane == 1, total(direction * image), jnp.where(
            lane == 2, total(residual * image), jnp.where(lane == 3, total(image * image), 0.0))))
    stat_col[0] = stats

    def tell_col(y):
        return pltpu.make_async_remote_copy(
            src_ref=stat_col.at[0], dst_ref=stat_col.at[y], send_sem=sc_send.at[y], recv_sem=sc_recv.at[y],
            device_id=device(down + y, across), device_id_type=MESH)

    def tell_row(x):
        return pltpu.make_async_remote_copy(
            src_ref=stat_row.at[0], dst_ref=stat_row.at[x], send_sem=sr_send.at[x], recv_sem=sr_recv.at[x],
            device_id=device(down, across + x), device_id_type=MESH)

    def hear_col(y, value):
        tell_col(y).wait_recv()
        return value + stat_col[y]

    def hear_row(x, value):
        tell_row(x).wait_recv()
        return value + stat_row[x]

    lax.fori_loop(1, SIDE, go(tell_col), 0)
    stats = lax.fori_loop(1, SIDE, hear_col, stats)
    stat_row[0] = stats
    lax.fori_loop(1, SIDE, go(tell_row), 0)
    stats = lax.fori_loop(1, SIDE, hear_row, stats)

    def pick(k):
        return jnp.sum(jnp.where(lane == k, stats, 0.0), axis=1, keepdims=True)

    rr, pap, cross, squared = pick(0), pick(1), pick(2), pick(3)
    alpha = rr / pap
    rr_next = jnp.maximum(rr - alpha * (2.0 * cross - alpha * squared), 0.0)
    res_next = residual - alpha * image
    sol_out[...] = sol_ref[...] + alpha * direction
    res_out[...] = res_next
    dir_out[...] = res_next + (rr_next / rr) * direction

    lax.fori_loop(1, SLOTS, sent(copy_row), 0)
    lax.fori_loop(1, SIDE, sent(copy_col), 0)
    lax.fori_loop(1, SLOTS, sent(give_row), 0)
    lax.fori_loop(1, SIDE, sent(give_col), 0)
    lax.fori_loop(1, SIDE, sent(tell_col), 0)
    lax.fori_loop(1, SIDE, sent(tell_row), 0)


def on_device(points, lengthscales, noise, solution, residual, direction):
    vmem = pl.BlockSpec(memory_space=pltpu.VMEM)
    smem = pl.BlockSpec(memory_space=pltpu.SMEM)
    out = jax.ShapeDtypeStruct((16, 256), F32)
    dma = pltpu.SemaphoreType.DMA
    return pl.pallas_call(
        kernel,
        out_shape=(out, out, out),
        in_specs=[smem, smem, vmem, vmem, vmem, vmem],
        out_specs=(vmem, vmem, vmem),
        scratch_shapes=[
            pltpu.VMEM((SLOTS, 32, 256), F32), pltpu.VMEM((SIDE, 32, 256), F32),
            pltpu.VMEM((SLOTS, 256, 128), BF16), pltpu.VMEM((SIDE, 128, 256), BF16),
            pltpu.VMEM((SLOTS, 32, 256), BF16), pltpu.VMEM((SIDE, 32, 256), BF16),
            pltpu.VMEM((SLOTS, 32, 256), F32), pltpu.VMEM((SIDE, 32, 256), F32),
            pltpu.VMEM((8, 256, 256), F32), pltpu.VMEM((8, 256, 256), BF16), pltpu.VMEM((8, 256, 256), BF16),
            pltpu.VMEM((SLOTS, 16, 256), F32), pltpu.VMEM((SIDE, 16, 256), F32),
            pltpu.VMEM((SLOTS, 16, 256), F32), pltpu.VMEM((SIDE, 16, 256), F32),
            pltpu.VMEM((SIDE, 16, 128), F32), pltpu.VMEM((SIDE, 16, 128), F32),
            dma((SLOTS,)), dma((SLOTS,)), dma((SIDE,)), dma((SIDE,)),
            dma((SLOTS,)), dma((SLOTS,)), dma((SIDE,)), dma((SIDE,)),
            dma((SIDE,)), dma((SIDE,)), dma((SIDE,)), dma((SIDE,)),
        ],
        compiler_params=pltpu.CompilerParams(
            collective_id=0, has_side_effects=True, vmem_limit_bytes=48 * 2**20),
    )(lengthscales, noise, points, solution, residual, direction)


def solution(mesh):
    placed = (P(None, "blk"), P(), P(), P(None, "blk"), P(None, "blk"), P(None, "blk"))
    return jax.shard_map(
        on_device,
        mesh=mesh,
        in_specs=placed,
        out_specs=(P(None, "blk"), P(None, "blk"), P(None, "blk")),
        check_vma=False,
    )
```

```python
import math

import jax
import jax.numpy as jnp
from jax import lax
from jax.experimental import pallas as pl
from jax.experimental.pallas import tpu as pltpu
from jax.sharding import PartitionSpec as P

MESH = pl.DeviceIdType.MESH
F32, BF16 = jnp.float32, jnp.bfloat16
SIDE = 16
SLOTS = 9
LN2 = math.log(2.0)
SCALE = math.sqrt(5.0) / LN2
CURVE = LN2 * LN2 / 3.0
BEND = 3.0 / LN2
LIFT = 3.0 / (LN2 * LN2)
LAST = (((1,), (1,)), ((), ()))


def three(value):
    high = value.astype(BF16).astype(F32)
    rest = value - high
    middle = rest.astype(BF16).astype(F32)
    return high, middle, (rest - middle).astype(BF16).astype(F32)


def two(value):
    high = value.astype(BF16)
    return high, (value - high.astype(F32)).astype(BF16)


def matern(square):
    square = jnp.maximum(square, 1e-30)
    root = square * lax.rsqrt(square)
    return (square + BEND * root + LIFT) * jnp.exp2(-root)


def kernel(
    scales_hbm, noise_hbm, points_hbm, sol_hbm, res_hbm, dir_hbm,
    sol_out, res_out, dir_out,
    scales_ref, noise_ref, points_ref, sol_ref, res_ref, dir_ref,
    rows, cols, left, right, dir_row, dir_col, acc_row, acc_col, square, high, low,
    out_row, out_col, in_row, in_col, stat_col, stat_row, load_sem,
    row_send, row_recv, col_send, col_recv, rs_row_send, rs_row_recv, rs_col_send, rs_col_recv,
    sc_send, sc_recv, sr_send, sr_recv,
):
    me = lax.axis_index("blk")
    down = lax.rem(me // 2, SIDE)
    across = (me // (2 * SIDE)) * 2 + lax.rem(me, 2)

    def device(i, l):
        i, l = lax.rem(i, SIDE), lax.rem(l, SIDE)
        return ((l // 2) * (2 * SIDE) + i * 2 + lax.rem(l, 2),)

    def step_of(slot):
        odd = lax.rem(slot, 2)
        return odd * slot + (1 - odd) * (SIDE - slot)

    loads = [
        pltpu.make_async_copy(a, b, load_sem.at[k])
        for k, (a, b) in enumerate((
            (points_hbm, points_ref), (scales_hbm, scales_ref), (dir_hbm, dir_ref),
            (noise_hbm, noise_ref), (sol_hbm, sol_ref), (res_hbm, res_ref)))
    ]
    for load in loads:
        load.start()
    barrier = pltpu.get_barrier_semaphore()

    def greet(k, _):
        pl.semaphore_signal(barrier, inc=1, device_id=device(down + k, across), device_id_type=MESH)
        pl.semaphore_signal(barrier, inc=1, device_id=device(down, across + k), device_id_type=MESH)
        return 0

    lax.fori_loop(1, SIDE, greet, 0)

    acc_row[...] = jnp.zeros_like(acc_row)
    acc_col[...] = jnp.zeros_like(acc_col)
    for load in loads:
        load.wait()

    line = lax.broadcasted_iota(jnp.int32, (SIDE, 256), 0)
    ratio = jnp.ones((SIDE, 256), F32)
    for f in range(11):
        ratio = jnp.where(line == f, scales_ref[f], ratio)
    cols[0, 0:16, :] = dir_ref[...]
    cols[0, 16:32, :] = jnp.zeros((16, 256), F32)
    cols[0, 16:27, :] = points_ref[...]
    feats = cols[0, 16:32, :] * (SCALE / ratio)
    norm = jnp.sum(feats * feats, axis=0, keepdims=True)
    block = jnp.where(line == 11, norm, jnp.where(line == 12, 1.0, feats))
    cols[0, 16:32, :] = block
    rows[0, 0:16, :] = dir_ref[...]
    rows[0, 16:32, :] = block

    pl.semaphore_wait(barrier, 2 * (SIDE - 1))

    def copy_row(s):
        return pltpu.make_async_remote_copy(
            src_ref=cols.at[0], dst_ref=rows.at[s], send_sem=row_send.at[s], recv_sem=row_recv.at[s],
            device_id=device(down, across + SIDE - step_of(s)), device_id_type=MESH)

    def copy_col(y):
        return pltpu.make_async_remote_copy(
            src_ref=cols.at[0], dst_ref=cols.at[y], send_sem=col_send.at[y], recv_sem=col_recv.at[y],
            device_id=device(down + SIDE - y, across), device_id_type=MESH)

    def go(make):
        def body(k, _):
            make(k).start()
            return 0
        return body

    def sent(make):
        def body(k, _):
            make(k).wait_send()
            return 0
        return body

    lax.fori_loop(1, 4, go(copy_row), 0)
    lax.fori_loop(1, 6, go(copy_col), 0)
    copy_row(8).start()
    lax.fori_loop(6, SIDE, go(copy_col), 0)
    lax.fori_loop(4, 8, go(copy_row), 0)


    def prep_row(s):
        dir_row[s] = jnp.concatenate(two(rows[s, 0:16, :]), axis=0)
        value = rows[s, 16:32, :]
        norm = jnp.sum(jnp.where(line == 11, value, 0.0), axis=0, keepdims=True)
        value = jnp.where(line == 11, 1.0, jnp.where(line == 12, norm, -2.0 * value))
        h, m, l = three(value)
        nil = jnp.zeros((SIDE, 256), F32)
        tall = jnp.concatenate([h, h, m, h, l, m, nil, nil], axis=0)
        left[s] = jnp.transpose(tall).astype(BF16)

    def prep_col(y):
        dir_col[y] = jnp.concatenate(two(cols[y, 0:16, :]), axis=0)
        h, m, l = three(cols[y, 16:32, :])
        nil = jnp.zeros((SIDE, 256), F32)
        right[y] = jnp.concatenate([h, m, h, l, h, m, nil, nil], axis=0).astype(BF16)

    prep_row(0)
    prep_col(0)

    def take_row(s):
        copy_row(s).wait_recv()
        prep_row(s)

    def take_col(y):
        copy_col(y).wait_recv()
        prep_col(y)

    def places(t):
        g, pair = t // 8, lax.rem(t, 8)
        upper = pair // 4
        first = g * 4 + (1 - g) * upper * 8
        slots = [first, g * 4 + 1, g * 4 + 2, g * 4 + 3]
        ys = [pair * 2, pair * 2 + 1]
        ys0 = [y - (1 - g) * upper * 8 for y in ys]
        return g, slots, ys, ys0

    def dot(a, b):
        return jnp.dot(a, b, preferred_element_type=F32)

    def dot_t(a, b):
        return lax.dot_general(a, b, LAST, preferred_element_type=F32)

    def distance(s, y):
        return dot(left[s], right[y])

    def work(t, apply, entries, distances, extra=()):
        g, slots, ys, ys0 = places(t - 2)
        _, slots_n, ys_n, ys0_n = places(t)
        one_way = jnp.where((g == 0) & (ys0[0] == 0), 0.0, 1.0).astype(F32)
        side_sum = [None, None]
        for s in extra:
            hi, lo = two(matern(distance(s, 8)))
            acc_row[s] += dot_t(dir_col[8], hi) + dot_t(dir_col[8], lo)
        for n in range(4):
            mine = None
            for j in range(2):
                k = n * 2 + j
                if apply:
                    hi, lo = high[k], low[k]
                    y = ys0[j] if n == 0 else ys[j]
                    term = dot_t(dir_col[y], hi) + dot_t(dir_col[y], lo)
                    mine = term if mine is None else mine + term
                    drow = dir_row[slots[n]]
                    term = dot(drow, hi) + dot(drow, lo)
                    if n == 0:
                        if j == 0:
                            term = term * one_way
                        acc_col[y] += term
                    else:
                        side_sum[j] = term if side_sum[j] is None else side_sum[j] + term
                if entries:
                    hi, lo = two(matern(square[k]))
                    high[k] = hi
                    low[k] = lo
                if distances:
                    y = ys0_n[j] if n == 0 else ys_n[j]
                    square[k] = distance(slots_n[n], y)
            if apply:
                acc_row[slots[n]] += mine
        if apply:
            for j in range(2):
                acc_col[ys[j]] += side_sum[j]

    def give_row(s):
        return pltpu.make_async_remote_copy(
            src_ref=out_row.at[s], dst_ref=in_row.at[s], send_sem=rs_row_send, recv_sem=rs_row_recv,
            device_id=device(down, across + step_of(s)), device_id_type=MESH)

    def give_col(y):
        return pltpu.make_async_remote_copy(
            src_ref=out_col.at[y], dst_ref=in_col.at[y], send_sem=rs_col_send, recv_sem=rs_col_recv,
            device_id=device(down + y, across), device_id_type=MESH)

    def push_row(s, _):
        out_row[s] = acc_row[s, 0:16, :] + acc_row[s, 16:32, :]
        give_row(s).start()
        return 0

    def push_col(y, _):
        out_col[y] = acc_col[y, 0:16, :] + acc_col[y, 16:32, :]
        give_col(y).start()
        return 0

    take_row(1)
    take_row(2)
    take_row(3)
    take_col(1)
    work(0, False, False, True)
    take_col(2)
    take_col(3)
    work(1, False, True, True)
    take_col(4)
    take_col(5)

    def early(t, _):
        s = jnp.where(t == 2, 8, t + 1)
        copy_row(s).wait_recv()
        copy_col(2 * t + 2).wait_recv()
        copy_col(2 * t + 3).wait_recv()
        prep_row(s)
        prep_col(2 * t + 2)
        prep_col(2 * t + 3)
        work(t, True, True, True)
        return 0

    def middle(t, _):
        work(t, True, True, True)
        return 0

    def late(t, _):
        push_col(2 * t - 22, 0)
        push_col(2 * t - 21, 0)
        work(t, True, True, True)
        return 0

    lax.fori_loop(2, 7, early, 0)
    lax.fori_loop(7, 11, middle, 0)
    lax.fori_loop(1, 4, push_row, 0)
    push_col(1, 0)
    work(11, True, True, True)
    lax.fori_loop(12, 16, late, 0)
    push_col(10, 0)
    push_col(11, 0)
    work(16, True, True, False, (0, 8))
    push_row(8, 0)
    push_col(12, 0)
    push_col(13, 0)
    work(17, True, False, False)
    push_col(14, 0)
    push_col(15, 0)
    lax.fori_loop(4, 8, push_row, 0)
    own = acc_row[0, 0:16, :] + acc_row[0, 16:32, :] + acc_col[0, 0:16, :] + acc_col[0, 16:32, :]

    def all_of(ref, sem):
        blocks = ref.at[pl.ds(1, ref.shape[0] - 1)]
        pltpu.make_async_copy(blocks, blocks, sem).wait()

    all_of(in_col, rs_col_recv)
    all_of(in_row, rs_row_recv)
    for s in range(1, SLOTS):
        own = own + in_row[s]
    for y in range(1, SIDE):
        own = own + in_col[y]
    direction = dir_ref[...]
    residual = res_ref[...]
    image = CURVE * own + noise_ref[0] * direction

    def total(value):
        return jnp.sum(value, axis=1, keepdims=True)

    lane = lax.broadcasted_iota(jnp.int32, (8, 128), 1)
    stats = jnp.zeros((8, 128), F32)
    for k, value in enumerate((residual * residual, direction * image, residual * image, image * image)):
        value = total(value)
        stats = jnp.where(lane == k, value[0:8], jnp.where(lane == k + 4, value[8:16], stats))
    stat_col[0] = stats

    def tell_col(y):
        return pltpu.make_async_remote_copy(
            src_ref=stat_col.at[0], dst_ref=stat_col.at[y], send_sem=sc_send, recv_sem=sc_recv,
            device_id=device(down + y, across), device_id_type=MESH)

    def tell_row(x):
        return pltpu.make_async_remote_copy(
            src_ref=stat_row.at[0], dst_ref=stat_row.at[x], send_sem=sr_send, recv_sem=sr_recv,
            device_id=device(down, across + x), device_id_type=MESH)

    for y in range(1, SIDE):
        tell_col(y).start()
    all_of(stat_col, sc_recv)
    for y in range(1, SIDE):
        stats = stats + stat_col[y]
    stat_row[0] = stats
    for x in range(1, SIDE):
        tell_row(x).start()
    all_of(stat_row, sr_recv)
    for x in range(1, SIDE):
        stats = stats + stat_row[x]

    def pick(k):
        return jnp.concatenate([total(jnp.where(lane == k + h, stats, 0.0)) for h in (0, 4)], axis=0)

    rr, pap, cross, squared = pick(0), pick(1), pick(2), pick(3)
    alpha = rr / pap
    rr_next = jnp.maximum(rr - alpha * (2.0 * cross - alpha * squared), 0.0)
    res_next = residual - alpha * image
    sol_out[...] = sol_ref[...] + alpha * direction
    res_out[...] = res_next
    dir_out[...] = res_next + (rr_next / rr) * direction

    lax.fori_loop(1, SLOTS, sent(copy_row), 0)
    lax.fori_loop(1, SIDE, sent(copy_col), 0)
    all_of(out_row, rs_row_send)
    all_of(out_col, rs_col_send)
    all_of(stat_col, sc_send)
    all_of(stat_row, sr_send)


def on_device(points, lengthscales, noise, solution, residual, direction):
    vmem = pl.BlockSpec(memory_space=pltpu.VMEM)
    out = jax.ShapeDtypeStruct((16, 256), F32)
    dma = pltpu.SemaphoreType.DMA
    return pl.pallas_call(
        kernel,
        out_shape=(out, out, out),
        in_specs=[pl.BlockSpec(memory_space=pltpu.HBM)] * 6,
        out_specs=(vmem, vmem, vmem),
        scratch_shapes=[
            pltpu.SMEM((11,), F32), pltpu.SMEM((1,), F32), pltpu.VMEM((11, 256), F32),
            pltpu.VMEM((16, 256), F32), pltpu.VMEM((16, 256), F32), pltpu.VMEM((16, 256), F32),
            pltpu.VMEM((SLOTS, 32, 256), F32), pltpu.VMEM((SIDE, 32, 256), F32),
            pltpu.VMEM((SLOTS, 256, 128), BF16), pltpu.VMEM((SIDE, 128, 256), BF16),
            pltpu.VMEM((SLOTS, 32, 256), BF16), pltpu.VMEM((SIDE, 32, 256), BF16),
            pltpu.VMEM((SLOTS, 32, 256), F32), pltpu.VMEM((SIDE, 32, 256), F32),
            pltpu.VMEM((8, 256, 256), F32), pltpu.VMEM((8, 256, 256), BF16), pltpu.VMEM((8, 256, 256), BF16),
            pltpu.VMEM((SLOTS, 16, 256), F32), pltpu.VMEM((SIDE, 16, 256), F32),
            pltpu.VMEM((SLOTS, 16, 256), F32), pltpu.VMEM((SIDE, 16, 256), F32),
            pltpu.VMEM((SIDE, 8, 128), F32), pltpu.VMEM((SIDE, 8, 128), F32), dma((6,)),
            dma((SLOTS,)), dma((SLOTS,)), dma((SIDE,)), dma((SIDE,)),
            dma, dma, dma, dma, dma, dma, dma, dma,
        ],
        compiler_params=pltpu.CompilerParams(
            collective_id=0, has_side_effects=True, vmem_limit_bytes=48 * 2**20),
    )(lengthscales, noise, points, solution, residual, direction)


def solution(mesh):
    placed = (P(None, "blk"), P(), P(), P(None, "blk"), P(None, "blk"), P(None, "blk"))
    return jax.shard_map(
        on_device,
        mesh=mesh,
        in_specs=placed,
        out_specs=(P(None, "blk"), P(None, "blk"), P(None, "blk")),
        check_vma=False,
    )
```

```python
import math

import jax
import jax.numpy as jnp
from jax import lax
from jax.experimental import pallas as pl
from jax.experimental.pallas import tpu as pltpu
from jax.sharding import PartitionSpec as P

MESH = pl.DeviceIdType.MESH
F32, BF16 = jnp.float32, jnp.bfloat16
SIDE = 16
PLACES = (4, 1, 7, 5, 12, 15, 13, 8, 11, 14, 9, 10, 6, 2, 3, 0)
OWN = SIDE - 1
SLOTS = 9
LN2 = math.log(2.0)
SCALE = math.sqrt(5.0) / LN2
CURVE = LN2 * LN2 / 3.0
BEND = 3.0 / LN2
LIFT = 3.0 / (LN2 * LN2)
LAST = (((1,), (1,)), ((), ()))


def three(value):
    high = value.astype(BF16).astype(F32)
    rest = value - high
    middle = rest.astype(BF16).astype(F32)
    return high, middle, (rest - middle).astype(BF16).astype(F32)


def two(value):
    high = value.astype(BF16)
    return high, (value - high.astype(F32)).astype(BF16)


def matern(square):
    square = jnp.maximum(square, 1e-30)
    root = square * lax.rsqrt(square)
    return (square + BEND * root + LIFT) * jnp.exp2(-root)


def kernel(
    scales_hbm, noise_hbm, points_hbm, sol_hbm, res_hbm, dir_hbm,
    out_ref,
    scales_ref, noise_ref, points_ref, sol_ref, res_ref, dir_ref,
    rows, cols, left, right, dir_row, dir_col, acc_row, acc_col, square, high, low,
    out_row, out_col, in_row, in_col, stat_col, stat_row, load_sem,
    row_send, row_recv, col_send, col_recv, rs_row_send, rs_row_recv, rs_col_send, rs_col_recv,
    sc_send, sc_recv, sr_send, sr_recv,
):
    me = lax.axis_index("blk")
    down = lax.rem(me // 2, SIDE)
    across = (me // (2 * SIDE)) * 2 + lax.rem(me, 2)

    def device(i, l):
        i, l = lax.rem(i, SIDE), lax.rem(l, SIDE)
        return ((l // 2) * (2 * SIDE) + i * 2 + lax.rem(l, 2),)

    def step_of(slot):
        odd = lax.rem(slot, 2)
        return odd * slot + (1 - odd) * (SIDE - slot)

    loads = [
        pltpu.make_async_copy(a, b, load_sem.at[k])
        for k, (a, b) in enumerate((
            (points_hbm, points_ref), (scales_hbm, scales_ref), (dir_hbm, dir_ref),
            (noise_hbm, noise_ref), (sol_hbm, sol_ref), (res_hbm, res_ref)))
    ]
    for load in loads:
        load.start()
    def offset_of(p):
        if isinstance(p, int):
            return PLACES[p]
        offset = PLACES[0]
        for k in range(1, SIDE):
            offset = jnp.where(p == k, PLACES[k], offset)
        return offset

    barrier = pltpu.get_barrier_semaphore()

    def greet(k, _):
        pl.semaphore_signal(barrier, inc=1, device_id=device(down + k, across), device_id_type=MESH)
        pl.semaphore_signal(barrier, inc=1, device_id=device(down, across + k), device_id_type=MESH)
        return 0

    lax.fori_loop(1, SIDE, greet, 0)

    acc_row[...] = jnp.zeros_like(acc_row)
    acc_col[...] = jnp.zeros_like(acc_col)
    for load in loads:
        load.wait()

    line = lax.broadcasted_iota(jnp.int32, (SIDE, 256), 0)
    ratio = jnp.ones((SIDE, 256), F32)
    for f in range(11):
        ratio = jnp.where(line == f, scales_ref[f], ratio)
    cols[OWN, 0:16, :] = dir_ref[...]
    cols[OWN, 16:32, :] = jnp.zeros((16, 256), F32)
    cols[OWN, 16:27, :] = points_ref[...]
    feats = cols[OWN, 16:32, :] * (SCALE / ratio)
    norm = jnp.sum(feats * feats, axis=0, keepdims=True)
    block = jnp.where(line == 11, norm, jnp.where(line == 12, 1.0, feats))
    cols[OWN, 16:32, :] = block
    rows[0, 0:16, :] = dir_ref[...]
    rows[0, 16:32, :] = block

    pl.semaphore_wait(barrier, 2 * (SIDE - 1))

    def copy_row(s):
        return pltpu.make_async_remote_copy(
            src_ref=cols.at[OWN], dst_ref=rows.at[s], send_sem=row_send, recv_sem=row_recv.at[s],
            device_id=device(down, across + SIDE - step_of(s)), device_id_type=MESH)

    def copy_col(p):
        return pltpu.make_async_remote_copy(
            src_ref=cols.at[OWN], dst_ref=cols.at[p], send_sem=col_send, recv_sem=col_recv.at[p],
            device_id=device(down + SIDE - offset_of(p), across), device_id_type=MESH)

    def arrived(ref, sem):
        pltpu.make_async_copy(ref, ref, sem).wait()

    for s in (1, 2, 3):
        copy_row(s).start()
    for p in range(0, 4):
        copy_col(p).start()
    copy_row(8).start()
    for p in range(4, 8):
        copy_col(p).start()
    for s in (4, 5, 6, 7):
        copy_row(s).start()
    for p in range(8, OWN):
        copy_col(p).start()

    def prep_row(s):
        dir_row[s] = jnp.concatenate(two(rows[s, 0:16, :]), axis=0)
        value = rows[s, 16:32, :]
        norm = jnp.sum(jnp.where(line == 11, value, 0.0), axis=0, keepdims=True)
        value = jnp.where(line == 11, 1.0, jnp.where(line == 12, norm, -2.0 * value))
        h, m, l = three(value)
        nil = jnp.zeros((SIDE, 256), F32)
        tall = jnp.concatenate([h, h, m, h, l, m, nil, nil], axis=0)
        left[s] = jnp.transpose(tall).astype(BF16)

    def prep_col(y):
        dir_col[y] = jnp.concatenate(two(cols[y, 0:16, :]), axis=0)
        h, m, l = three(cols[y, 16:32, :])
        nil = jnp.zeros((SIDE, 256), F32)
        right[y] = jnp.concatenate([h, m, h, l, h, m, nil, nil], axis=0).astype(BF16)

    prep_row(0)
    prep_col(OWN)

    def take_row(s):
        arrived(rows.at[s], row_recv.at[s])
        prep_row(s)

    def take_col(p):
        arrived(cols.at[p], col_recv.at[p])
        prep_col(p)

    def places(t):
        near = jnp.where((t < 4) | (t >= 12), 1, 0)
        pair = jnp.where(t < 4, t, jnp.where(t < 12, t - 4, t - 8))
        first = jnp.where(near == 0, 4, jnp.where((pair >= 2) & (pair <= 5), 8, 0))
        base = 4 * (1 - near)
        return near, pair, [first, base + 1, base + 2, base + 3]

    def dot(a, b):
        return jnp.dot(a, b, preferred_element_type=F32)

    def dot_t(a, b):
        return lax.dot_general(a, b, LAST, preferred_element_type=F32)

    def distance(s, y):
        return dot(left[s], right[y])

    def spread(d, hi, lo, product):
        both, rest = product(d, hi), product(d[0:16], lo)
        return jnp.concatenate([both[0:16] + rest, both[16:32]], axis=0)

    def leftover(s, p):
        hi, lo = two(matern(distance(s, p)))
        acc_row[s] += spread(dir_col[p], hi, lo, dot_t)

    def work(t, apply, entries, distances):
        near, pair, slots = places(t - 2)
        _, pair_n, slots_n = places(t)
        one_way = jnp.where((near == 1) & ((pair == 3) | (pair == 7)), 0.0, 1.0).astype(F32)
        side_sum = [None, None]
        for n in range(4):
            mine = None
            for j in range(2):
                k = n * 2 + j
                if apply:
                    hi, lo = high[k], low[k]
                    term = spread(dir_col[pair * 2 + j], hi, lo, dot_t)
                    mine = term if mine is None else mine + term
                    term = spread(dir_row[slots[n]], hi, lo, dot)
                    if n == 0 and j == 1:
                        term = term * one_way
                    side_sum[j] = term if side_sum[j] is None else side_sum[j] + term
                if entries:
                    hi, lo = two(matern(square[k]))
                    high[k] = hi
                    low[k] = lo
                if distances:
                    square[k] = distance(slots_n[n], pair_n * 2 + j)
            if apply:
                acc_row[slots[n]] += mine
        if apply:
            for j in range(2):
                acc_col[pair * 2 + j] += side_sum[j]

    def give_row(s):
        return pltpu.make_async_remote_copy(
            src_ref=out_row.at[s], dst_ref=in_row.at[s], send_sem=rs_row_send, recv_sem=rs_row_recv,
            device_id=device(down, across + step_of(s)), device_id_type=MESH)

    def give_col(p):
        return pltpu.make_async_remote_copy(
            src_ref=out_col.at[p], dst_ref=in_col.at[p], send_sem=rs_col_send, recv_sem=rs_col_recv,
            device_id=device(down + offset_of(p), across), device_id_type=MESH)

    def push_row(s):
        out_row[s] = acc_row[s, 0:16, :] + acc_row[s, 16:32, :]
        give_row(s).start()

    def push_col(p):
        out_col[p] = acc_col[p, 0:16, :] + acc_col[p, 16:32, :]
        give_col(p).start()

    take_row(1)
    take_row(2)
    take_row(3)
    take_col(0)
    take_col(1)
    work(0, False, False, True)
    take_col(2)
    take_col(3)
    work(1, False, True, True)

    def early(t, _):
        @pl.when(t == 2)
        def _():
            take_row(8)

        @pl.when(t == 3)
        def _():
            for s in (4, 5, 6, 7):
                arrived(rows.at[s], row_recv.at[s])
            for s in (4, 5, 6, 7):
                prep_row(s)

        for j in range(2):
            arrived(cols.at[2 * t + j], col_recv.at[2 * t + j])
        for j in range(2):
            prep_col(2 * t + j)
        work(t, True, True, True)
        return 0

    def late(t, _):
        @pl.when((t <= 10) | (t == 15))
        def _():
            p = jnp.where(t == 15, 8, 2 * t - 14)
            push_col(p)
            push_col(p + 1)

        @pl.when(t == 14)
        def _():
            for s in (4, 5, 6, 7):
                push_row(s)

        work(t, True, True, True)
        return 0

    lax.fori_loop(2, 7, early, 0)
    arrived(cols.at[14], col_recv.at[14])
    prep_col(14)
    leftover(0, 7)
    leftover(8, OWN)
    lax.fori_loop(7, 16, late, 0)
    push_col(10)
    push_col(11)
    push_row(8)
    work(16, True, True, False)
    push_col(12)
    push_col(13)
    work(17, True, False, False)
    for s in (3, 2, 1):
        push_row(s)
    push_col(14)
    own = acc_row[0, 0:16, :] + acc_row[0, 16:32, :] + acc_col[OWN, 0:16, :] + acc_col[OWN, 16:32, :]

    arrived(in_col.at[pl.ds(0, SIDE - 1)], rs_col_recv)
    for p in range(SIDE - 1):
        own = own + in_col[p]
    arrived(in_row.at[pl.ds(1, SLOTS - 1)], rs_row_recv)
    for s in range(1, SLOTS):
        own = own + in_row[s]
    direction = dir_ref[...]
    residual = res_ref[...]
    image = CURVE * own + noise_ref[0] * direction

    def total(value):
        return jnp.sum(value, axis=1, keepdims=True)

    lane = lax.broadcasted_iota(jnp.int32, (8, 128), 1)
    stats = jnp.zeros((8, 128), F32)
    for k, value in enumerate((residual * residual, direction * image, residual * image, image * image)):
        value = total(value)
        stats = jnp.where(lane == k, value[0:8], jnp.where(lane == k + 4, value[8:16], stats))
    stat_col[0] = stats

    def tell_col(y):
        return pltpu.make_async_remote_copy(
            src_ref=stat_col.at[0], dst_ref=stat_col.at[y], send_sem=sc_send, recv_sem=sc_recv,
            device_id=device(down + y, across), device_id_type=MESH)

    def tell_row(x):
        return pltpu.make_async_remote_copy(
            src_ref=stat_row.at[0], dst_ref=stat_row.at[x], send_sem=sr_send, recv_sem=sr_recv,
            device_id=device(down, across + x), device_id_type=MESH)

    for y in range(1, SIDE):
        tell_col(y).start()
    arrived(stat_col.at[pl.ds(1, SIDE - 1)], sc_recv)
    for y in range(1, SIDE):
        stats = stats + stat_col[y]
    stat_row[0] = stats
    for x in range(1, SIDE):
        tell_row(x).start()
    arrived(stat_row.at[pl.ds(1, SIDE - 1)], sr_recv)
    for x in range(1, SIDE):
        stats = stats + stat_row[x]

    def pick(k):
        return jnp.concatenate([total(jnp.where(lane == k + h, stats, 0.0)) for h in (0, 4)], axis=0)

    rr, pap, cross, squared = pick(0), pick(1), pick(2), pick(3)
    alpha = rr / pap
    rr_next = jnp.maximum(rr - alpha * (2.0 * cross - alpha * squared), 0.0)
    out_ref[0:16, :] = image
    out_ref[16:32, :] = jnp.broadcast_to(alpha, (16, 256))
    out_ref[32:48, :] = jnp.broadcast_to(rr_next / rr, (16, 256))

    arrived(rows.at[pl.ds(1, SLOTS - 1)], row_send)
    arrived(cols.at[pl.ds(0, SIDE - 1)], col_send)
    arrived(out_row.at[pl.ds(1, SLOTS - 1)], rs_row_send)
    arrived(out_col.at[pl.ds(0, SIDE - 1)], rs_col_send)
    arrived(stat_col.at[pl.ds(1, SIDE - 1)], sc_send)
    arrived(stat_row.at[pl.ds(1, SIDE - 1)], sr_send)


def on_device(points, lengthscales, noise, solution, residual, direction):
    vmem = pl.BlockSpec(memory_space=pltpu.VMEM)
    out = jax.ShapeDtypeStruct((16, 256), F32)
    dma = pltpu.SemaphoreType.DMA
    packed = pl.pallas_call(
        kernel,
        out_shape=jax.ShapeDtypeStruct((48, 256), F32),
        in_specs=[pl.BlockSpec(memory_space=pltpu.HBM)] * 6,
        out_specs=vmem,
        scratch_shapes=[
            pltpu.SMEM((11,), F32), pltpu.SMEM((1,), F32), pltpu.VMEM((11, 256), F32),
            pltpu.VMEM((16, 256), F32), pltpu.VMEM((16, 256), F32), pltpu.VMEM((16, 256), F32),
            pltpu.VMEM((SLOTS, 32, 256), F32), pltpu.VMEM((SIDE, 32, 256), F32),
            pltpu.VMEM((SLOTS, 256, 128), BF16), pltpu.VMEM((SIDE, 128, 256), BF16),
            pltpu.VMEM((SLOTS, 32, 256), BF16), pltpu.VMEM((SIDE, 32, 256), BF16),
            pltpu.VMEM((SLOTS, 32, 256), F32), pltpu.VMEM((SIDE, 32, 256), F32),
            pltpu.VMEM((8, 256, 256), F32), pltpu.VMEM((8, 256, 256), BF16), pltpu.VMEM((8, 256, 256), BF16),
            pltpu.VMEM((SLOTS, 16, 256), F32), pltpu.VMEM((SIDE, 16, 256), F32),
            pltpu.VMEM((SLOTS, 16, 256), F32), pltpu.VMEM((SIDE, 16, 256), F32),
            pltpu.VMEM((SIDE, 8, 128), F32), pltpu.VMEM((SIDE, 8, 128), F32), dma((6,)),
            dma, dma((SLOTS,)), dma, dma((SIDE,)),
            dma, dma, dma, dma, dma, dma, dma, dma,
        ],
        compiler_params=pltpu.CompilerParams(
            collective_id=0, has_side_effects=True, vmem_limit_bytes=60 * 2**20),
    )(lengthscales, noise, points, solution, residual, direction)
    image, alpha, beta = packed[0:16], packed[16:32], packed[32:48]
    residual_next = residual - alpha * image
    return solution + alpha * direction, residual_next, residual_next + beta * direction


def solution(mesh):
    placed = (P(None, "blk"), P(), P(), P(None, "blk"), P(None, "blk"), P(None, "blk"))
    return jax.shard_map(
        on_device,
        mesh=mesh,
        in_specs=placed,
        out_specs=(P(None, "blk"), P(None, "blk"), P(None, "blk")),
        check_vma=False,
    )
```

```python
import math

import jax
import jax.numpy as jnp
from jax import lax
from jax.experimental import pallas as pl
from jax.experimental.pallas import tpu as pltpu
from jax.sharding import PartitionSpec as P

MESH = pl.DeviceIdType.MESH
F32, BF16 = jnp.float32, jnp.bfloat16
SIDE = 16
PLACES = (4, 1, 7, 5, 12, 15, 13, 8, 11, 14, 9, 10, 6, 2, 3, 0)
OWN = SIDE - 1
STEPS = (0, 15, 2, 13, 12, 5, 10, 7, 8)
SLOTS = 9
LN2 = math.log(2.0)
SCALE = math.sqrt(5.0) / LN2
CURVE = LN2 * LN2 / 3.0
BEND = 3.0 / LN2
LIFT = 3.0 / (LN2 * LN2)
LAST = (((1,), (1,)), ((), ()))


def three(value):
    high = value.astype(BF16).astype(F32)
    rest = value - high
    middle = rest.astype(BF16).astype(F32)
    return high, middle, (rest - middle).astype(BF16).astype(F32)


def two(value):
    high = value.astype(BF16)
    return high, (value - high.astype(F32)).astype(BF16)


def matern(square):
    square = jnp.maximum(square, 1e-30)
    root = square * lax.rsqrt(square)
    return (square + BEND * root + LIFT) * jnp.exp2(-root)


def kernel(
    scales_hbm, noise_hbm, points_hbm, sol_hbm, res_hbm, dir_hbm,
    out_ref,
    scales_ref, noise_ref, points_ref, sol_ref, res_ref, dir_ref,
    rows, cols, left, right, dir_row, dir_col, acc_row, acc_col, square, high, low,
    out_row, out_col, in_row, in_col, stat_col, stat_row, load_sem,
    row_send, row_near, row_recv, col_send, col_near, col_recv, rs_row_send, rs_row_recv, rs_col_send, rs_col_recv,
    sc_send, sc_recv, sr_send, sr_recv,
):
    me = lax.axis_index("blk")
    down = lax.rem(me // 2, SIDE)
    across = (me // (2 * SIDE)) * 2 + lax.rem(me, 2)

    def device(i, l):
        i, l = lax.rem(i, SIDE), lax.rem(l, SIDE)
        return ((l // 2) * (2 * SIDE) + i * 2 + lax.rem(l, 2),)

    def offset_of(p):
        if isinstance(p, int):
            return PLACES[p]
        offset = PLACES[0]
        for k in range(1, SIDE):
            offset = jnp.where(p == k, PLACES[k], offset)
        return offset

    barrier = pltpu.get_barrier_semaphore()

    def greet(k, _):
        pl.semaphore_signal(barrier, inc=1, device_id=device(down + k, across), device_id_type=MESH)
        pl.semaphore_signal(barrier, inc=1, device_id=device(down, across + k), device_id_type=MESH)
        return 0

    lax.fori_loop(1, SIDE, greet, 0)
    loads = [
        pltpu.make_async_copy(a, b, load_sem.at[k])
        for k, (a, b) in enumerate((
            (points_hbm, points_ref), (scales_hbm, scales_ref), (dir_hbm, dir_ref),
            (noise_hbm, noise_ref), (sol_hbm, sol_ref), (res_hbm, res_ref)))
    ]
    for load in loads:
        load.start()

    acc_row[...] = jnp.zeros_like(acc_row)
    acc_col[...] = jnp.zeros_like(acc_col)
    for load in loads:
        load.wait()

    line = lax.broadcasted_iota(jnp.int32, (SIDE, 256), 0)
    ratio = jnp.ones((SIDE, 256), F32)
    for f in range(11):
        ratio = jnp.where(line == f, scales_ref[f], ratio)
    cols[OWN, 0:16, :] = dir_ref[...]
    cols[OWN, 16:32, :] = jnp.zeros((16, 256), F32)
    cols[OWN, 16:27, :] = points_ref[...]
    feats = cols[OWN, 16:32, :] * (SCALE / ratio)
    norm = jnp.sum(feats * feats, axis=0, keepdims=True)
    block = jnp.where(line == 11, norm, jnp.where(line == 12, 1.0, feats))
    cols[OWN, 16:32, :] = block
    rows[0, 0:16, :] = dir_ref[...]
    rows[0, 16:32, :] = block

    pl.semaphore_wait(barrier, 2 * (SIDE - 1))

    FEATS, DIRS = pl.ds(16, 16), pl.ds(0, 16)

    def copy_row(s, part):
        return pltpu.make_async_remote_copy(
            src_ref=cols.at[OWN, part], dst_ref=rows.at[s, part], send_sem=row_send,
            recv_sem=(row_near if part is FEATS else row_recv).at[s],
            device_id=device(down, across + SIDE - STEPS[s]), device_id_type=MESH)

    def copy_col(p, part):
        return pltpu.make_async_remote_copy(
            src_ref=cols.at[OWN, part], dst_ref=cols.at[p, part], send_sem=col_send,
            recv_sem=(col_near if part is FEATS else col_recv).at[p],
            device_id=device(down + SIDE - offset_of(p), across), device_id_type=MESH)

    def arrived(ref, sem):
        pltpu.make_async_copy(ref, ref, sem).wait()

    def ship(*lots):
        for make, part, ids in lots:
            for k in ids:
                make(k, part).start()

    ship((copy_row, FEATS, (1, 2, 3)), (copy_col, FEATS, (0, 1, 2, 3)), (copy_row, DIRS, (1, 2, 3)), (copy_row, FEATS, (8,)), (copy_col, FEATS, (4, 5, 6, 7)), (copy_col, DIRS, (0, 1, 2, 3)), (copy_row, FEATS, (6, 7, 4, 5)), (copy_col, FEATS, (8, 9, 10, 11)), (copy_row, DIRS, (8,)), (copy_col, DIRS, (4, 5, 6, 7)),)

    def prep_row(s):
        value = rows[s, 16:32, :]
        norm = jnp.sum(jnp.where(line == 11, value, 0.0), axis=0, keepdims=True)
        value = jnp.where(line == 11, 1.0, jnp.where(line == 12, norm, -2.0 * value))
        h, m, l = three(value)
        nil = jnp.zeros((SIDE, 256), F32)
        tall = jnp.concatenate([h, h, m, h, l, m, nil, nil], axis=0)
        left[s] = jnp.transpose(tall).astype(BF16)

    def prep_col(p):
        h, m, l = three(cols[p, 16:32, :])
        nil = jnp.zeros((SIDE, 256), F32)
        right[p] = jnp.concatenate([h, m, h, l, h, m, nil, nil], axis=0).astype(BF16)

    def take_row(s):
        arrived(rows.at[s, FEATS], row_near.at[s])
        prep_row(s)

    def take_col(p):
        arrived(cols.at[p, FEATS], col_near.at[p])
        prep_col(p)

    def take_row_dir(s):
        arrived(rows.at[s, DIRS], row_recv.at[s])
        dir_row[s] = jnp.concatenate(two(rows[s, 0:16, :]), axis=0)

    def take_col_dir(p):
        arrived(cols.at[p, DIRS], col_recv.at[p])
        dir_col[p] = jnp.concatenate(two(cols[p, 0:16, :]), axis=0)

    prep_row(0)
    prep_col(OWN)
    own_dir = jnp.concatenate(two(dir_ref[...]), axis=0)
    dir_row[0] = own_dir
    dir_col[OWN] = own_dir

    def places(t):
        near = jnp.where((t < 6) | (t >= 14), 1, 0)
        pair = jnp.where(t < 6, t, jnp.maximum(t - 8, 0))
        quad = jnp.where(t < 10, t - 6, t - 10)
        base = jnp.where(t < 10, 6, 4)
        first = jnp.where((pair >= 2) & (pair <= 5), 8, 0)
        slots, spots = [], []
        for n in range(4):
            slots.append(jnp.where(near == 1, n if n else first, base + n // 2))
            spots.append([jnp.where(near == 1, 2 * pair + j, 4 * quad + n % 2 * 2 + j) for j in range(2)])
        return near, pair, slots, spots

    def dot(a, b):
        return jnp.dot(a, b, preferred_element_type=F32)

    def dot_t(a, b):
        return lax.dot_general(a, b, LAST, preferred_element_type=F32)

    def distance(s, y):
        return dot(left[s], right[y])

    def spread(d, hi, lo, product):
        both, rest = product(d, hi), product(d[0:16], lo)
        return jnp.concatenate([both[0:16] + rest, both[16:32]], axis=0)

    def work(t, apply, entries, distances):
        near, pair, slots, spots = places(t - 2)
        _, _, slots_n, spots_n = places(t)
        one_way = jnp.where((near == 1) & ((pair == 3) | (pair == 7)), 0.0, 1.0).astype(F32)
        for n in range(4):
            mine = None
            for j in range(2):
                k = n * 2 + j
                if apply:
                    hi, lo = high[k], low[k]
                    term = spread(dir_col[spots[n][j]], hi, lo, dot_t)
                    mine = term if mine is None else mine + term
                    term = spread(dir_row[slots[n]], hi, lo, dot)
                    if n == 0 and j == 1:
                        term = term * one_way
                    acc_col[spots[n][j]] += term
                if entries:
                    hi, lo = two(matern(square[k]))
                    high[k] = hi
                    low[k] = lo
                if distances:
                    square[k] = distance(slots_n[n], spots_n[n][j])
            if apply:
                acc_row[slots[n]] += mine

    def give_row(s):
        return pltpu.make_async_remote_copy(
            src_ref=out_row.at[s], dst_ref=in_row.at[s], send_sem=rs_row_send, recv_sem=rs_row_recv,
            device_id=device(down, across + STEPS[s]), device_id_type=MESH)

    def give_col(p):
        return pltpu.make_async_remote_copy(
            src_ref=out_col.at[p], dst_ref=in_col.at[p], send_sem=rs_col_send, recv_sem=rs_col_recv,
            device_id=device(down + offset_of(p), across), device_id_type=MESH)

    def push_row(s):
        out_row[s] = acc_row[s, 0:16, :] + acc_row[s, 16:32, :]
        give_row(s).start()

    def push_col(p):
        out_col[p] = acc_col[p, 0:16, :] + acc_col[p, 16:32, :]
        give_col(p).start()

    for s in (1, 2, 3):
        take_row(s)
    take_col(0)
    take_col(1)
    work(0, False, False, True)
    take_col(2)
    take_col(3)
    work(1, False, True, True)

    def early(t, _):
        @pl.when(t == 2)
        def _():
            take_row(8)
            for s in (1, 2, 3):
                take_row_dir(s)

        @pl.when(t == 3)
        def _():
            ship((copy_row, DIRS, (6, 7, 4, 5)), (copy_col, DIRS, (8, 9, 10, 11)), (copy_col, FEATS, (12, 13, 14)), (copy_col, DIRS, (12, 13, 14)),)

        @pl.when(t == 4)
        def _():
            take_row_dir(8)

        @pl.when(t == 6)
        def _():
            for s in (4, 5, 6, 7):
                take_row(s)

        take_col_dir(2 * t - 4)
        take_col_dir(2 * t - 3)
        arrived(cols.at[2 * t, FEATS], col_near.at[2 * t])

        @pl.when(t <= 6)
        def _():
            arrived(cols.at[2 * t + 1, FEATS], col_near.at[2 * t + 1])

        for j in range(2):
            prep_col(2 * t + j)
        work(t, True, True, True)
        return 0

    def late(t, _):
        @pl.when(t == 12)
        def _():
            push_row(7)
            push_row(6)

        @pl.when(t >= 13)
        def _():
            for k in range(4):
                push_col(4 * t - 52 + k)

        work(t, True, True, True)
        return 0

    lax.fori_loop(2, 8, early, 0)
    for s in (4, 5, 6, 7):
        take_row_dir(s)
    for p in (12, 13, 14):
        take_col_dir(p)
    push_row(8)
    lax.fori_loop(8, 16, late, 0)
    push_row(5)
    push_row(4)
    work(16, True, True, False)
    push_col(12)
    push_col(13)
    work(17, True, False, False)
    for s in (3, 2, 1):
        push_row(s)
    push_col(14)
    extra = spread(dir_col[7], *two(matern(distance(0, 7))), dot_t)
    extra = extra + spread(dir_row[8], *two(matern(distance(8, OWN))), dot)
    extra = extra + acc_row[0] + acc_col[OWN]
    own = extra[0:16] + extra[16:32]

    arrived(in_col.at[pl.ds(0, SIDE - 1)], rs_col_recv)
    for p in range(SIDE - 1):
        own = own + in_col[p]
    arrived(in_row.at[pl.ds(1, SLOTS - 1)], rs_row_recv)
    for s in range(1, SLOTS):
        own = own + in_row[s]
    direction = dir_ref[...]
    residual = res_ref[...]
    image = CURVE * own + noise_ref[0] * direction

    def total(value):
        return jnp.sum(value, axis=1, keepdims=True)

    lane = lax.broadcasted_iota(jnp.int32, (16, 128), 1) - lax.broadcasted_iota(jnp.int32, (16, 128), 0)
    stats = jnp.zeros((16, 128), F32)
    for k, value in enumerate((residual * residual, direction * image, residual * image, image * image)):
        stats = jnp.where(lane == 16 * k, total(value), stats)
    stats = jnp.sum(stats, axis=0, keepdims=True)
    stat_col[0:1, :] = stats

    def tell_col(y):
        return pltpu.make_async_remote_copy(
            src_ref=stat_col.at[pl.ds(0, 1)], dst_ref=stat_col.at[pl.ds(y, 1)], send_sem=sc_send, recv_sem=sc_recv,
            device_id=device(down + y, across), device_id_type=MESH)

    def tell_row(x):
        return pltpu.make_async_remote_copy(
            src_ref=stat_row.at[pl.ds(0, 1)], dst_ref=stat_row.at[pl.ds(x, 1)], send_sem=sr_send, recv_sem=sr_recv,
            device_id=device(down, across + x), device_id_type=MESH)

    for y in range(1, SIDE):
        tell_col(y).start()
    arrived(stat_col.at[pl.ds(1, SIDE - 1)], sc_recv)
    stats = jnp.sum(stat_col[...], axis=0, keepdims=True)
    stat_row[0:1, :] = stats
    for x in range(1, SIDE):
        tell_row(x).start()
    arrived(stat_row.at[pl.ds(1, SIDE - 1)], sr_recv)
    stats = jnp.sum(stat_row[...], axis=0, keepdims=True)

    def pick(k):
        return total(jnp.where(lane == 16 * k, stats, 0.0))

    rr, pap, cross, squared = pick(0), pick(1), pick(2), pick(3)
    alpha = rr / pap
    rr_next = jnp.maximum(rr - alpha * (2.0 * cross - alpha * squared), 0.0)
    out_ref[0:16, :] = image
    out_ref[16:32, :] = jnp.broadcast_to(alpha, (16, 256))
    out_ref[32:48, :] = jnp.broadcast_to(rr_next / rr, (16, 256))

    arrived(rows.at[pl.ds(1, SLOTS - 1)], row_send)
    arrived(cols.at[pl.ds(0, SIDE - 1)], col_send)
    arrived(out_row.at[pl.ds(1, SLOTS - 1)], rs_row_send)
    arrived(out_col.at[pl.ds(0, SIDE - 1)], rs_col_send)
    arrived(stat_col.at[pl.ds(1, SIDE - 1)], sc_send)
    arrived(stat_row.at[pl.ds(1, SIDE - 1)], sr_send)


def on_device(points, lengthscales, noise, solution, residual, direction):
    vmem = pl.BlockSpec(memory_space=pltpu.VMEM)
    out = jax.ShapeDtypeStruct((16, 256), F32)
    dma = pltpu.SemaphoreType.DMA
    packed = pl.pallas_call(
        kernel,
        out_shape=jax.ShapeDtypeStruct((48, 256), F32),
        in_specs=[pl.BlockSpec(memory_space=pltpu.HBM)] * 6,
        out_specs=vmem,
        scratch_shapes=[
            pltpu.SMEM((11,), F32), pltpu.SMEM((1,), F32), pltpu.VMEM((11, 256), F32),
            pltpu.VMEM((16, 256), F32), pltpu.VMEM((16, 256), F32), pltpu.VMEM((16, 256), F32),
            pltpu.VMEM((SLOTS, 32, 256), F32), pltpu.VMEM((SIDE, 32, 256), F32),
            pltpu.VMEM((SLOTS, 256, 128), BF16), pltpu.VMEM((SIDE, 128, 256), BF16),
            pltpu.VMEM((SLOTS, 32, 256), BF16), pltpu.VMEM((SIDE, 32, 256), BF16),
            pltpu.VMEM((SLOTS, 32, 256), F32), pltpu.VMEM((SIDE, 32, 256), F32),
            pltpu.VMEM((8, 256, 256), F32), pltpu.VMEM((8, 256, 256), BF16), pltpu.VMEM((8, 256, 256), BF16),
            pltpu.VMEM((SLOTS, 16, 256), F32), pltpu.VMEM((SIDE, 16, 256), F32),
            pltpu.VMEM((SLOTS, 16, 256), F32), pltpu.VMEM((SIDE, 16, 256), F32),
            pltpu.VMEM((SIDE, 128), F32), pltpu.VMEM((SIDE, 128), F32), dma((6,)),
            dma, dma((SLOTS,)), dma((SLOTS,)), dma, dma((SIDE,)), dma((SIDE,)),
            dma, dma, dma, dma, dma, dma, dma, dma,
        ],
        compiler_params=pltpu.CompilerParams(
            collective_id=0, has_side_effects=True, vmem_limit_bytes=60 * 2**20),
    )(lengthscales, noise, points, solution, residual, direction)
    image, alpha, beta = packed[0:16], packed[16:32], packed[32:48]
    residual_next = residual - alpha * image
    return solution + alpha * direction, residual_next, residual_next + beta * direction


def solution(mesh):
    placed = (P(None, "blk"), P(), P(), P(None, "blk"), P(None, "blk"), P(None, "blk"))
    return jax.shard_map(
        on_device,
        mesh=mesh,
        in_specs=placed,
        out_specs=(P(None, "blk"), P(None, "blk"), P(None, "blk")),
        check_vma=False,
    )
```

```python
import math

import jax
import jax.numpy as jnp
from jax import lax
from jax.experimental import pallas as pl
from jax.experimental.pallas import tpu as pltpu
from jax.sharding import PartitionSpec as P

MESH = pl.DeviceIdType.MESH
F32, BF16 = jnp.float32, jnp.bfloat16
SIDE = 16
PLACES = (4, 1, 7, 5, 12, 15, 13, 8, 11, 14, 9, 10, 6, 2, 3, 0)
OWN = SIDE - 1
FAR = sorted(
    ((z, x, y) for z in range(8) for x in range(4) for y in range(4) if z + x + y),
    key=lambda d: -(min(d[0], 8 - d[0]) + min(d[1], 4 - d[1]) + min(d[2], 4 - d[2])))
STEPS = (0, 15, 2, 13, 12, 5, 10, 7, 8)
SLOTS = 9
LN2 = math.log(2.0)
SCALE = math.sqrt(5.0) / LN2
CURVE = LN2 * LN2 / 3.0
BEND = 3.0 / LN2
LIFT = 3.0 / (LN2 * LN2)
LAST = (((1,), (1,)), ((), ()))


def three(value):
    high = value.astype(BF16).astype(F32)
    rest = value - high
    middle = rest.astype(BF16).astype(F32)
    return high, middle, (rest - middle).astype(BF16).astype(F32)


def two(value):
    high = value.astype(BF16)
    return high, (value - high.astype(F32)).astype(BF16)


def matern(square):
    square = jnp.maximum(square, 1e-30)
    root = square * lax.rsqrt(square)
    return (square + BEND * root + LIFT) * jnp.exp2(-root)


def kernel(
    scales_hbm, noise_hbm, points_hbm, sol_hbm, res_hbm, dir_hbm,
    out_ref,
    scales_ref, noise_ref, points_ref, sol_ref, res_ref, dir_ref,
    rows, cols, left, right, dir_row, dir_col, acc_row, acc_col, square, high, low,
    out_row, out_col, in_row, in_col, pair_stat, chip_stat, load_sem,
    row_send, row_near, row_recv, col_send, col_near, col_recv, rs_row_send, rs_row_recv, rs_col_send, rs_col_recv,
    sc_send, sc_recv, sr_send, sr_recv,
):
    me = lax.axis_index("blk")
    down = lax.rem(me // 2, SIDE)
    across = (me // (2 * SIDE)) * 2 + lax.rem(me, 2)

    def device(i, l):
        i, l = lax.rem(i, SIDE), lax.rem(l, SIDE)
        return ((l // 2) * (2 * SIDE) + i * 2 + lax.rem(l, 2),)

    def offset_of(p):
        if isinstance(p, int):
            return PLACES[p]
        offset = PLACES[0]
        for k in range(1, SIDE):
            offset = jnp.where(p == k, PLACES[k], offset)
        return offset

    barrier = pltpu.get_barrier_semaphore()

    def greet(k, _):
        pl.semaphore_signal(barrier, inc=1, device_id=device(down + k, across), device_id_type=MESH)
        pl.semaphore_signal(barrier, inc=1, device_id=device(down, across + k), device_id_type=MESH)
        return 0

    lax.fori_loop(1, SIDE, greet, 0)
    loads = [
        pltpu.make_async_copy(a, b, load_sem.at[k])
        for k, (a, b) in enumerate((
            (points_hbm, points_ref), (scales_hbm, scales_ref), (dir_hbm, dir_ref),
            (noise_hbm, noise_ref), (sol_hbm, sol_ref), (res_hbm, res_ref)))
    ]
    for load in loads:
        load.start()

    acc_row[...] = jnp.zeros_like(acc_row)
    acc_col[...] = jnp.zeros_like(acc_col)
    for load in loads:
        load.wait()

    line = lax.broadcasted_iota(jnp.int32, (SIDE, 256), 0)
    ratio = jnp.ones((SIDE, 256), F32)
    for f in range(11):
        ratio = jnp.where(line == f, scales_ref[f], ratio)
    cols[OWN, 0:16, :] = dir_ref[...]
    cols[OWN, 16:32, :] = jnp.zeros((16, 256), F32)
    cols[OWN, 16:27, :] = points_ref[...]
    feats = cols[OWN, 16:32, :] * (SCALE / ratio)
    norm = jnp.sum(feats * feats, axis=0, keepdims=True)
    block = jnp.where(line == 11, norm, jnp.where(line == 12, 1.0, feats))
    cols[OWN, 16:32, :] = block
    rows[0, 0:16, :] = dir_ref[...]
    rows[0, 16:32, :] = block

    pl.semaphore_wait(barrier, 2 * (SIDE - 1))

    FEATS, DIRS = pl.ds(16, 16), pl.ds(0, 16)

    def copy_row(s, part):
        return pltpu.make_async_remote_copy(
            src_ref=cols.at[OWN, part], dst_ref=rows.at[s, part], send_sem=row_send,
            recv_sem=(row_near if part is FEATS else row_recv).at[s],
            device_id=device(down, across + SIDE - STEPS[s]), device_id_type=MESH)

    def copy_col(p, part):
        return pltpu.make_async_remote_copy(
            src_ref=cols.at[OWN, part], dst_ref=cols.at[p, part], send_sem=col_send,
            recv_sem=(col_near if part is FEATS else col_recv).at[p],
            device_id=device(down + SIDE - offset_of(p), across), device_id_type=MESH)

    def arrived(ref, sem):
        pltpu.make_async_copy(ref, ref, sem).wait()

    def ship(*lots):
        for make, part, ids in lots:
            for k in ids:
                make(k, part).start()

    ship((copy_row, FEATS, (1, 2, 3)), (copy_col, FEATS, (0, 1, 2, 3)), (copy_row, DIRS, (1, 2, 3)), (copy_row, FEATS, (8,)), (copy_col, FEATS, (4, 5, 6, 7)), (copy_col, DIRS, (0, 1, 2, 3)), (copy_row, FEATS, (6, 7, 4, 5)), (copy_col, FEATS, (8, 9, 10, 11)), (copy_row, DIRS, (8,)), (copy_col, DIRS, (4, 5, 6, 7)),)

    def prep_row(s):
        value = rows[s, 16:32, :]
        norm = jnp.sum(jnp.where(line == 11, value, 0.0), axis=0, keepdims=True)
        value = jnp.where(line == 11, 1.0, jnp.where(line == 12, norm, -2.0 * value))
        h, m, l = three(value)
        nil = jnp.zeros((SIDE, 256), F32)
        tall = jnp.concatenate([h, h, m, h, l, m, nil, nil], axis=0)
        left[s] = jnp.transpose(tall).astype(BF16)

    def prep_col(p):
        h, m, l = three(cols[p, 16:32, :])
        nil = jnp.zeros((SIDE, 256), F32)
        right[p] = jnp.concatenate([h, m, h, l, h, m, nil, nil], axis=0).astype(BF16)

    def take_row(s):
        arrived(rows.at[s, FEATS], row_near.at[s])
        prep_row(s)

    def take_col(p):
        arrived(cols.at[p, FEATS], col_near.at[p])
        prep_col(p)

    def take_row_dir(s):
        arrived(rows.at[s, DIRS], row_recv.at[s])
        dir_row[s] = jnp.concatenate(two(rows[s, 0:16, :]), axis=0)

    def take_col_dir(p):
        arrived(cols.at[p, DIRS], col_recv.at[p])
        dir_col[p] = jnp.concatenate(two(cols[p, 0:16, :]), axis=0)

    prep_row(0)
    prep_col(OWN)
    own_dir = jnp.concatenate(two(dir_ref[...]), axis=0)
    dir_row[0] = own_dir
    dir_col[OWN] = own_dir

    def places(t):
        near = jnp.where((t < 6) | (t >= 14), 1, 0)
        pair = jnp.where(t < 6, t, jnp.maximum(t - 8, 0))
        quad = jnp.where(t < 10, t - 6, t - 10)
        base = jnp.where(t < 10, 6, 4)
        first = jnp.where((pair >= 2) & (pair <= 5), 8, 0)
        slots, spots = [], []
        for n in range(4):
            slots.append(jnp.where(near == 1, n if n else first, base + n // 2))
            spots.append([jnp.where(near == 1, 2 * pair + j, 4 * quad + n % 2 * 2 + j) for j in range(2)])
        return near, pair, slots, spots

    def dot(a, b):
        return jnp.dot(a, b, preferred_element_type=F32)

    def dot_t(a, b):
        return lax.dot_general(a, b, LAST, preferred_element_type=F32)

    def distance(s, y):
        return dot(left[s], right[y])

    def spread(d, hi, lo, product):
        both, rest = product(d, hi), product(d[0:16], lo)
        return jnp.concatenate([both[0:16] + rest, both[16:32]], axis=0)

    def work(t, apply, entries, distances):
        near, pair, slots, spots = places(t - 2)
        _, _, slots_n, spots_n = places(t)
        one_way = jnp.where((near == 1) & ((pair == 3) | (pair == 7)), 0.0, 1.0).astype(F32)
        for n in range(4):
            mine = None
            for j in range(2):
                k = n * 2 + j
                if apply:
                    hi, lo = high[k], low[k]
                    term = spread(dir_col[spots[n][j]], hi, lo, dot_t)
                    mine = term if mine is None else mine + term
                    term = spread(dir_row[slots[n]], hi, lo, dot)
                    if n == 0 and j == 1:
                        term = term * one_way
                    acc_col[spots[n][j]] += term
                if entries:
                    hi, lo = two(matern(square[k]))
                    high[k] = hi
                    low[k] = lo
                if distances:
                    square[k] = distance(slots_n[n], spots_n[n][j])
            if apply:
                acc_row[slots[n]] += mine

    def give_row(s):
        return pltpu.make_async_remote_copy(
            src_ref=out_row.at[s], dst_ref=in_row.at[s], send_sem=rs_row_send, recv_sem=rs_row_recv,
            device_id=device(down, across + STEPS[s]), device_id_type=MESH)

    def give_col(p):
        return pltpu.make_async_remote_copy(
            src_ref=out_col.at[p], dst_ref=in_col.at[p], send_sem=rs_col_send, recv_sem=rs_col_recv,
            device_id=device(down + offset_of(p), across), device_id_type=MESH)

    def push_row(s):
        out_row[s] = acc_row[s, 0:16, :] + acc_row[s, 16:32, :]
        give_row(s).start()

    def push_col(p):
        out_col[p] = acc_col[p, 0:16, :] + acc_col[p, 16:32, :]
        give_col(p).start()

    for s in (1, 2, 3):
        take_row(s)
    take_col(0)
    take_col(1)
    work(0, False, False, True)
    take_col(2)
    take_col(3)
    work(1, False, True, True)

    def early(t, _):
        @pl.when(t == 2)
        def _():
            take_row(8)
            for s in (1, 2, 3):
                take_row_dir(s)

        @pl.when(t == 3)
        def _():
            ship((copy_row, DIRS, (6, 7, 4, 5)), (copy_col, DIRS, (8, 9, 10, 11)), (copy_col, FEATS, (12, 13, 14)), (copy_col, DIRS, (12, 13, 14)),)

        @pl.when(t == 4)
        def _():
            take_row_dir(8)

        @pl.when(t == 6)
        def _():
            for s in (4, 5, 6, 7):
                take_row(s)

        take_col_dir(2 * t - 4)
        take_col_dir(2 * t - 3)
        arrived(cols.at[2 * t, FEATS], col_near.at[2 * t])

        @pl.when(t <= 6)
        def _():
            arrived(cols.at[2 * t + 1, FEATS], col_near.at[2 * t + 1])

        for j in range(2):
            prep_col(2 * t + j)
        work(t, True, True, True)
        return 0

    def late(t, _):
        @pl.when(t == 12)
        def _():
            push_row(7)
            push_row(6)

        @pl.when(t >= 13)
        def _():
            for k in range(4):
                push_col(4 * t - 52 + k)

        work(t, True, True, True)
        return 0

    lax.fori_loop(2, 8, early, 0)
    for s in (4, 5, 6, 7):
        take_row_dir(s)
    for p in (12, 13, 14):
        take_col_dir(p)
    push_row(8)
    lax.fori_loop(8, 16, late, 0)
    push_row(5)
    push_row(4)
    work(16, True, True, False)
    push_col(12)
    push_col(13)
    work(17, True, False, False)
    for s in (3, 2, 1):
        push_row(s)
    push_col(14)
    extra = spread(dir_col[7], *two(matern(distance(0, 7))), dot_t)
    extra = extra + spread(dir_row[8], *two(matern(distance(8, OWN))), dot)
    extra = extra + acc_row[0] + acc_col[OWN]
    own = extra[0:16] + extra[16:32]

    arrived(in_col.at[pl.ds(0, SIDE - 1)], rs_col_recv)
    for p in range(SIDE - 1):
        own = own + in_col[p]
    arrived(in_row.at[pl.ds(1, SLOTS - 1)], rs_row_recv)
    for s in range(1, SLOTS):
        own = own + in_row[s]
    direction = dir_ref[...]
    residual = res_ref[...]
    image = CURVE * own + noise_ref[0] * direction

    def total(value):
        return jnp.sum(value, axis=1, keepdims=True)

    lane = lax.broadcasted_iota(jnp.int32, (16, 128), 1) - lax.broadcasted_iota(jnp.int32, (16, 128), 0)
    stats = jnp.zeros((16, 128), F32)
    for k, value in enumerate((residual * residual, direction * image, residual * image, image * image)):
        stats = jnp.where(lane == 16 * k, total(value), stats)
    stats = jnp.sum(stats, axis=0, keepdims=True)

    core = lax.rem(me, 2)
    pair_stat[0:1, :] = stats
    tell_core = pltpu.make_async_remote_copy(
        src_ref=pair_stat.at[pl.ds(0, 1)], dst_ref=pair_stat.at[pl.ds(8, 1)], send_sem=sc_send, recv_sem=sc_recv,
        device_id=(me + 1 - 2 * core,), device_id_type=MESH)
    tell_core.start()
    zs = [lax.rem(me // 32 + d, 8) * 32 + core for d in range(8)]
    xs = [lax.rem(me // 8 + d, 4) * 8 for d in range(4)]
    ys = [lax.rem(me // 2 + d, 4) * 2 for d in range(4)]
    tell_core.wait_recv()
    chip_stat[0:1, :] = stats + pair_stat[8:9, :]
    for k, (dz, dx, dy) in enumerate(FAR):
        pltpu.make_async_remote_copy(
            src_ref=chip_stat.at[pl.ds(0, 1)], dst_ref=chip_stat.at[pl.ds(k + 1, 1)],
            send_sem=sr_send, recv_sem=sr_recv,
            device_id=(zs[dz] + xs[dx] + ys[dy],), device_id_type=MESH).start()
    others = chip_stat.at[pl.ds(1, len(FAR))]
    arrived(others, sr_recv)
    stats = jnp.sum(chip_stat[...], axis=0, keepdims=True)

    def pick(k):
        return total(jnp.where(lane == 16 * k, stats, 0.0))

    rr, pap, cross, squared = pick(0), pick(1), pick(2), pick(3)
    alpha = rr / pap
    rr_next = jnp.maximum(rr - alpha * (2.0 * cross - alpha * squared), 0.0)
    out_ref[0:16, :] = image
    out_ref[16:32, :] = jnp.broadcast_to(alpha, (16, 256))
    out_ref[32:48, :] = jnp.broadcast_to(rr_next / rr, (16, 256))

    arrived(rows.at[pl.ds(1, SLOTS - 1)], row_send)
    arrived(cols.at[pl.ds(0, SIDE - 1)], col_send)
    arrived(out_row.at[pl.ds(1, SLOTS - 1)], rs_row_send)
    arrived(out_col.at[pl.ds(0, SIDE - 1)], rs_col_send)
    tell_core.wait_send()
    arrived(others, sr_send)


def on_device(points, lengthscales, noise, solution, residual, direction):
    vmem = pl.BlockSpec(memory_space=pltpu.VMEM)
    out = jax.ShapeDtypeStruct((16, 256), F32)
    dma = pltpu.SemaphoreType.DMA
    packed = pl.pallas_call(
        kernel,
        out_shape=jax.ShapeDtypeStruct((48, 256), F32),
        in_specs=[pl.BlockSpec(memory_space=pltpu.HBM)] * 6,
        out_specs=vmem,
        scratch_shapes=[
            pltpu.SMEM((11,), F32), pltpu.SMEM((1,), F32), pltpu.VMEM((11, 256), F32),
            pltpu.VMEM((16, 256), F32), pltpu.VMEM((16, 256), F32), pltpu.VMEM((16, 256), F32),
            pltpu.VMEM((SLOTS, 32, 256), F32), pltpu.VMEM((SIDE, 32, 256), F32),
            pltpu.VMEM((SLOTS, 256, 128), BF16), pltpu.VMEM((SIDE, 128, 256), BF16),
            pltpu.VMEM((SLOTS, 32, 256), BF16), pltpu.VMEM((SIDE, 32, 256), BF16),
            pltpu.VMEM((SLOTS, 32, 256), F32), pltpu.VMEM((SIDE, 32, 256), F32),
            pltpu.VMEM((8, 256, 256), F32), pltpu.VMEM((8, 256, 256), BF16), pltpu.VMEM((8, 256, 256), BF16),
            pltpu.VMEM((SLOTS, 16, 256), F32), pltpu.VMEM((SIDE, 16, 256), F32),
            pltpu.VMEM((SLOTS, 16, 256), F32), pltpu.VMEM((SIDE, 16, 256), F32),
            pltpu.VMEM((16, 128), F32), pltpu.VMEM((128, 128), F32), dma((6,)),
            dma, dma((SLOTS,)), dma((SLOTS,)), dma, dma((SIDE,)), dma((SIDE,)),
            dma, dma, dma, dma, dma, dma, dma, dma,
        ],
        compiler_params=pltpu.CompilerParams(
            collective_id=0, has_side_effects=True, vmem_limit_bytes=60 * 2**20),
    )(lengthscales, noise, points, solution, residual, direction)
    image, alpha, beta = packed[0:16], packed[16:32], packed[32:48]
    residual_next = residual - alpha * image
    return solution + alpha * direction, residual_next, residual_next + beta * direction


def solution(mesh):
    placed = (P(None, "blk"), P(), P(), P(None, "blk"), P(None, "blk"), P(None, "blk"))
    return jax.shard_map(
        on_device,
        mesh=mesh,
        in_specs=placed,
        out_specs=(P(None, "blk"), P(None, "blk"), P(None, "blk")),
        check_vma=False,
    )
```

```python
import math

import jax
import jax.numpy as jnp
from jax import lax
from jax.experimental import pallas as pl
from jax.experimental.pallas import tpu as pltpu
from jax.sharding import PartitionSpec as P

MESH = pl.DeviceIdType.MESH
F32, BF16 = jnp.float32, jnp.bfloat16
SIDE = 16
PLACES = (4, 1, 7, 5, 12, 15, 13, 8, 11, 14, 9, 10, 6, 2, 3, 0)
OWN = SIDE - 1
FAR = sorted(
    ((z, x, y) for z in range(8) for x in range(4) for y in range(4) if z + x + y),
    key=lambda d: -(min(d[0], 8 - d[0]) + min(d[1], 4 - d[1]) + min(d[2], 4 - d[2])))
STEPS = (0, 15, 2, 13, 12, 5, 10, 7, 8)
SLOTS = 9
LN2 = math.log(2.0)
SCALE = math.sqrt(5.0) / LN2
CURVE = LN2 * LN2 / 3.0
BEND = 3.0 / LN2
LIFT = 3.0 / (LN2 * LN2)
LAST = (((1,), (1,)), ((), ()))


def three(value):
    high = value.astype(BF16).astype(F32)
    rest = value - high
    middle = rest.astype(BF16).astype(F32)
    return high, middle, (rest - middle).astype(BF16).astype(F32)


def two(value):
    high = value.astype(BF16)
    return high, (value - high.astype(F32)).astype(BF16)


def matern(square):
    square = jnp.maximum(square, 1e-30)
    root = square * lax.rsqrt(square)
    return (square + BEND * root + LIFT) * jnp.exp2(-root)


def kernel(
    scales_hbm, noise_hbm, points_hbm, res_hbm, dir_hbm,
    out_ref,
    scales_ref, noise_ref, points_ref, res_ref, dir_ref,
    rows, cols, left, right, dir_row, dir_col, acc_row, acc_col, square, high, low,
    out_row, out_col, in_row, in_col, pair_stat, chip_stat, load_sem,
    row_send, row_near, row_recv, col_send, col_near, col_recv, rs_row_send, rs_row_recv, rs_col_send, rs_col_recv,
    sc_send, sc_recv, sr_send, sr_recv,
):
    me = lax.axis_index("blk")
    down = lax.rem(me // 2, SIDE)
    across = (me // (2 * SIDE)) * 2 + lax.rem(me, 2)

    def device(i, l):
        i, l = lax.rem(i, SIDE), lax.rem(l, SIDE)
        return ((l // 2) * (2 * SIDE) + i * 2 + lax.rem(l, 2),)

    def offset_of(p):
        if isinstance(p, int):
            return PLACES[p]
        offset = PLACES[0]
        for k in range(1, SIDE):
            offset = jnp.where(p == k, PLACES[k], offset)
        return offset

    barrier = pltpu.get_barrier_semaphore()

    def greet(k, _):
        pl.semaphore_signal(barrier, inc=1, device_id=device(down + k, across), device_id_type=MESH)
        pl.semaphore_signal(barrier, inc=1, device_id=device(down, across + k), device_id_type=MESH)
        return 0

    lax.fori_loop(1, SIDE, greet, 0)
    loads = [
        pltpu.make_async_copy(a, b, load_sem.at[k])
        for k, (a, b) in enumerate((
            (points_hbm, points_ref), (scales_hbm, scales_ref), (dir_hbm, dir_ref),
            (noise_hbm, noise_ref), (res_hbm, res_ref)))
    ]
    for load in loads:
        load.start()

    acc_row[...] = jnp.zeros_like(acc_row)
    acc_col[...] = jnp.zeros_like(acc_col)
    for load in loads:
        load.wait()

    line = lax.broadcasted_iota(jnp.int32, (SIDE, 256), 0)
    ratio = jnp.ones((SIDE, 256), F32)
    for f in range(11):
        ratio = jnp.where(line == f, scales_ref[f], ratio)
    cols[OWN, 0:16, :] = dir_ref[...]
    cols[OWN, 16:32, :] = jnp.zeros((16, 256), F32)
    cols[OWN, 16:27, :] = points_ref[...]
    feats = cols[OWN, 16:32, :] * (SCALE / ratio)
    norm = jnp.sum(feats * feats, axis=0, keepdims=True)
    block = jnp.where(line == 11, norm, jnp.where(line == 12, 1.0, feats))
    cols[OWN, 16:32, :] = block
    rows[0, 0:16, :] = dir_ref[...]
    rows[0, 16:32, :] = block

    pl.semaphore_wait(barrier, 2 * (SIDE - 1))

    FEATS, DIRS = pl.ds(16, 16), pl.ds(0, 16)

    def copy_row(s, part):
        return pltpu.make_async_remote_copy(
            src_ref=cols.at[OWN, part], dst_ref=rows.at[s, part], send_sem=row_send,
            recv_sem=(row_near if part is FEATS else row_recv).at[s],
            device_id=device(down, across + SIDE - STEPS[s]), device_id_type=MESH)

    def copy_col(p, part):
        return pltpu.make_async_remote_copy(
            src_ref=cols.at[OWN, part], dst_ref=cols.at[p, part], send_sem=col_send,
            recv_sem=(col_near if part is FEATS else col_recv).at[p],
            device_id=device(down + SIDE - offset_of(p), across), device_id_type=MESH)

    def arrived(ref, sem):
        pltpu.make_async_copy(ref, ref, sem).wait()

    def ship(*lots):
        for make, part, ids in lots:
            for k in ids:
                make(k, part).start()

    ship((copy_row, FEATS, (1, 2, 3)), (copy_col, FEATS, (0, 1, 2, 3)), (copy_row, DIRS, (1, 2, 3)), (copy_row, FEATS, (8,)), (copy_col, FEATS, (4, 5, 6, 7)), (copy_col, DIRS, (0, 1, 2, 3)), (copy_row, FEATS, (6, 7, 4, 5)), (copy_col, FEATS, (8, 9, 10, 11)), (copy_row, DIRS, (8,)), (copy_col, DIRS, (4, 5, 6, 7)),)

    def prep_row(s):
        value = rows[s, 16:32, :]
        norm = jnp.sum(jnp.where(line == 11, value, 0.0), axis=0, keepdims=True)
        value = jnp.where(line == 11, 1.0, jnp.where(line == 12, norm, -2.0 * value))
        h, m, l = three(value)
        tall = jnp.concatenate([h, h, m, h, l, m], axis=0)
        left[s] = jnp.transpose(tall).astype(BF16)

    def prep_col(p):
        h, m, l = three(cols[p, 16:32, :])
        right[p] = jnp.concatenate([h, m, h, l, h, m], axis=0).astype(BF16)

    def take_row(s):
        arrived(rows.at[s, FEATS], row_near.at[s])
        prep_row(s)

    def take_col(p):
        arrived(cols.at[p, FEATS], col_near.at[p])
        prep_col(p)

    def take_row_dir(s):
        arrived(rows.at[s, DIRS], row_recv.at[s])
        dir_row[s] = jnp.concatenate(two(rows[s, 0:16, :]), axis=0)

    def split_col_dir(p):
        dir_col[p] = jnp.concatenate(two(cols[p, 0:16, :]), axis=0)

    def take_col_dir(p):
        arrived(cols.at[p, DIRS], col_recv.at[p])
        split_col_dir(p)

    prep_row(0)
    prep_col(OWN)
    own_dir = jnp.concatenate(two(dir_ref[...]), axis=0)
    dir_row[0] = own_dir
    dir_col[OWN] = own_dir

    def places(t):
        near = jnp.where((t < 6) | (t >= 14), 1, 0)
        pair = jnp.where(t < 6, t, jnp.maximum(t - 8, 0))
        quad = jnp.where(t < 10, t - 6, t - 10)
        base = jnp.where(t < 10, 6, 4)
        first = jnp.where((pair >= 2) & (pair <= 5), 8, 0)
        slots, spots = [], []
        for n in range(4):
            slots.append(jnp.where(near == 1, n if n else first, base + n // 2))
            spots.append([jnp.where(near == 1, 2 * pair + j, 4 * quad + n % 2 * 2 + j) for j in range(2)])
        return near, pair, slots, spots

    def dot(a, b):
        return jnp.dot(a, b, preferred_element_type=F32)

    def dot_t(a, b):
        return lax.dot_general(a, b, LAST, preferred_element_type=F32)

    def distance(s, y):
        return dot(left[s], right[y])

    def spread(d, hi, lo, product):
        both, rest = product(d, hi), product(d[0:16], lo)
        return jnp.concatenate([both[0:16] + rest, both[16:32]], axis=0)

    def work(t, apply, entries, distances):
        near, pair, slots, spots = places(t - 2)
        _, _, slots_n, spots_n = places(t)
        one_way = jnp.where((near == 1) & ((pair == 3) | (pair == 7)), 0.0, 1.0).astype(F32)
        for n in range(4):
            mine = None
            for j in range(2):
                k = n * 2 + j
                if apply:
                    hi, lo = high[k], low[k]
                    term = spread(dir_col[spots[n][j]], hi, lo, dot_t)
                    mine = term if mine is None else mine + term
                    term = spread(dir_row[slots[n]], hi, lo, dot)
                    if n == 0 and j == 1:
                        term = term * one_way
                    acc_col[spots[n][j]] += term
                if entries:
                    hi, lo = two(matern(square[k]))
                    high[k] = hi
                    low[k] = lo
                if distances:
                    square[k] = distance(slots_n[n], spots_n[n][j])
            if apply:
                acc_row[slots[n]] += mine

    def give_row(s):
        return pltpu.make_async_remote_copy(
            src_ref=out_row.at[s], dst_ref=in_row.at[s], send_sem=rs_row_send, recv_sem=rs_row_recv,
            device_id=device(down, across + STEPS[s]), device_id_type=MESH)

    def give_col(p):
        return pltpu.make_async_remote_copy(
            src_ref=out_col.at[p], dst_ref=in_col.at[p], send_sem=rs_col_send, recv_sem=rs_col_recv,
            device_id=device(down + offset_of(p), across), device_id_type=MESH)

    def push_row(s):
        out_row[s] = acc_row[s, 0:16, :] + acc_row[s, 16:32, :]
        give_row(s).start()

    def push_col(p):
        out_col[p] = acc_col[p, 0:16, :] + acc_col[p, 16:32, :]
        give_col(p).start()

    for s in (1, 2, 3):
        take_row(s)
    take_col(0)
    take_col(1)
    work(0, False, False, True)
    take_col(2)
    take_col(3)
    work(1, False, True, True)

    def early(t, _):
        @pl.when(t == 2)
        def _():
            take_row(8)
            for s in (1, 2, 3):
                take_row_dir(s)

        @pl.when(t == 3)
        def _():
            ship((copy_row, DIRS, (6, 7, 4, 5)), (copy_col, DIRS, (8, 9, 10, 11)), (copy_col, FEATS, (12, 13, 14)), (copy_col, DIRS, (12, 13, 14)),)

        @pl.when(t == 4)
        def _():
            take_row_dir(8)

        @pl.when(t == 6)
        def _():
            for s in (4, 5, 6, 7):
                take_row(s)

        for j in range(2):
            arrived(cols.at[2 * t - 4 + j, DIRS], col_recv.at[2 * t - 4 + j])
        arrived(cols.at[2 * t, FEATS], col_near.at[2 * t])

        @pl.when(t <= 6)
        def _():
            arrived(cols.at[2 * t + 1, FEATS], col_near.at[2 * t + 1])

        for j in range(2):
            split_col_dir(2 * t - 4 + j)
            prep_col(2 * t + j)
        work(t, True, True, True)
        return 0

    def late(t, _):
        @pl.when(t == 12)
        def _():
            push_row(7)
            push_row(6)

        @pl.when(t >= 13)
        def _():
            for k in range(4):
                push_col(4 * t - 52 + k)

        work(t, True, True, True)
        return 0

    lax.fori_loop(2, 8, early, 0)
    for s in (4, 5, 6, 7):
        take_row_dir(s)
    for p in (12, 13, 14):
        take_col_dir(p)
    push_row(8)
    lax.fori_loop(8, 16, late, 0)
    push_row(5)
    push_row(4)
    work(16, True, True, False)
    push_col(12)
    push_col(13)
    work(17, True, False, False)
    for s in (3, 2, 1):
        push_row(s)
    push_col(14)
    extra = spread(dir_col[7], *two(matern(distance(0, 7))), dot_t)
    extra = extra + spread(dir_row[8], *two(matern(distance(8, OWN))), dot)
    extra = extra + acc_row[0] + acc_col[OWN]
    own = extra[0:16] + extra[16:32]

    arrived(in_col.at[pl.ds(0, SIDE - 1)], rs_col_recv)
    for p in range(SIDE - 1):
        own = own + in_col[p]
    arrived(in_row.at[pl.ds(1, SLOTS - 1)], rs_row_recv)
    for s in range(1, SLOTS):
        own = own + in_row[s]
    direction = dir_ref[...]
    residual = res_ref[...]
    image = CURVE * own + noise_ref[0] * direction

    def total(value):
        return jnp.sum(value, axis=1, keepdims=True)

    lane = lax.broadcasted_iota(jnp.int32, (16, 128), 1) - lax.broadcasted_iota(jnp.int32, (16, 128), 0)
    stats = jnp.zeros((16, 128), F32)
    for k, value in enumerate((residual * residual, direction * image, residual * image, image * image)):
        stats = jnp.where(lane == 16 * k, total(value), stats)
    stats = jnp.sum(stats, axis=0, keepdims=True)

    core = lax.rem(me, 2)
    pair_stat[0:1, :] = stats
    tell_core = pltpu.make_async_remote_copy(
        src_ref=pair_stat.at[pl.ds(0, 1)], dst_ref=pair_stat.at[pl.ds(8, 1)], send_sem=sc_send, recv_sem=sc_recv,
        device_id=(me + 1 - 2 * core,), device_id_type=MESH)
    tell_core.start()
    zs = [lax.rem(me // 32 + d, 8) * 32 + core for d in range(8)]
    xs = [lax.rem(me // 8 + d, 4) * 8 for d in range(4)]
    ys = [lax.rem(me // 2 + d, 4) * 2 for d in range(4)]
    tell_core.wait_recv()
    chip_stat[0:1, :] = stats + pair_stat[8:9, :]
    for k, (dz, dx, dy) in enumerate(FAR):
        pltpu.make_async_remote_copy(
            src_ref=chip_stat.at[pl.ds(0, 1)], dst_ref=chip_stat.at[pl.ds(k + 1, 1)],
            send_sem=sr_send, recv_sem=sr_recv,
            device_id=(zs[dz] + xs[dx] + ys[dy],), device_id_type=MESH).start()
    others = chip_stat.at[pl.ds(1, len(FAR))]
    arrived(others, sr_recv)
    stats = jnp.sum(chip_stat[...], axis=0, keepdims=True)

    def pick(k):
        return total(jnp.where(lane == 16 * k, stats, 0.0))

    rr, pap, cross, squared = pick(0), pick(1), pick(2), pick(3)
    alpha = rr / pap
    rr_next = jnp.maximum(rr - alpha * (2.0 * cross - alpha * squared), 0.0)
    out_ref[0:16, :] = image
    out_ref[16:32, :] = jnp.broadcast_to(alpha, (16, 256))
    out_ref[32:48, :] = jnp.broadcast_to(rr_next / rr, (16, 256))

    arrived(rows.at[pl.ds(1, SLOTS - 1)], row_send)
    arrived(cols.at[pl.ds(0, SIDE - 1)], col_send)
    arrived(out_row.at[pl.ds(1, SLOTS - 1)], rs_row_send)
    arrived(out_col.at[pl.ds(0, SIDE - 1)], rs_col_send)
    tell_core.wait_send()
    arrived(others, sr_send)


def on_device(points, lengthscales, noise, solution, residual, direction):
    vmem = pl.BlockSpec(memory_space=pltpu.VMEM)
    out = jax.ShapeDtypeStruct((16, 256), F32)
    dma = pltpu.SemaphoreType.DMA
    packed = pl.pallas_call(
        kernel,
        out_shape=jax.ShapeDtypeStruct((48, 256), F32),
        in_specs=[pl.BlockSpec(memory_space=pltpu.HBM)] * 5,
        out_specs=vmem,
        scratch_shapes=[
            pltpu.SMEM((11,), F32), pltpu.SMEM((1,), F32), pltpu.VMEM((11, 256), F32),
            pltpu.VMEM((16, 256), F32), pltpu.VMEM((16, 256), F32),
            pltpu.VMEM((SLOTS, 32, 256), F32), pltpu.VMEM((SIDE, 32, 256), F32),
            pltpu.VMEM((SLOTS, 256, 96), BF16), pltpu.VMEM((SIDE, 96, 256), BF16),
            pltpu.VMEM((SLOTS, 32, 256), BF16), pltpu.VMEM((SIDE, 32, 256), BF16),
            pltpu.VMEM((SLOTS, 32, 256), F32), pltpu.VMEM((SIDE, 32, 256), F32),
            pltpu.VMEM((8, 256, 256), F32), pltpu.VMEM((8, 256, 256), BF16), pltpu.VMEM((8, 256, 256), BF16),
            pltpu.VMEM((SLOTS, 16, 256), F32), pltpu.VMEM((SIDE, 16, 256), F32),
            pltpu.VMEM((SLOTS, 16, 256), F32), pltpu.VMEM((SIDE, 16, 256), F32),
            pltpu.VMEM((16, 128), F32), pltpu.VMEM((128, 128), F32), dma((5,)),
            dma, dma((SLOTS,)), dma((SLOTS,)), dma, dma((SIDE,)), dma((SIDE,)),
            dma, dma, dma, dma, dma, dma, dma, dma,
        ],
        compiler_params=pltpu.CompilerParams(
            collective_id=0, has_side_effects=True, vmem_limit_bytes=60 * 2**20),
    )(lengthscales, noise, points, residual, direction)
    image, alpha, beta = packed[0:16], packed[16:32], packed[32:48]
    residual_next = residual - alpha * image
    return solution + alpha * direction, residual_next, residual_next + beta * direction


def solution(mesh):
    placed = (P(None, "blk"), P(), P(), P(None, "blk"), P(None, "blk"), P(None, "blk"))
    return jax.shard_map(
        on_device,
        mesh=mesh,
        in_specs=placed,
        out_specs=(P(None, "blk"), P(None, "blk"), P(None, "blk")),
        check_vma=False,
    )
```

```python
import math

import jax
import jax.numpy as jnp
from jax import lax
from jax.experimental import pallas as pl
from jax.experimental.pallas import tpu as pltpu
from jax.sharding import PartitionSpec as P

MESH = pl.DeviceIdType.MESH
F32, BF16 = jnp.float32, jnp.bfloat16
SIDE = 16
PLACES = (4, 1, 7, 6, 12, 15, 13, 8, 11, 14, 9, 10, 5, 2, 3, 0)
OWN = SIDE - 1
FAR = sorted(
    ((z, x, y) for z in range(8) for x in range(4) for y in range(4) if z + x + y),
    key=lambda d: -(min(d[0], 8 - d[0]) + min(d[1], 4 - d[1]) + min(d[2], 4 - d[2])))
STEPS = (0, 15, 2, 13, 12, 5, 10, 7, 8)
SLOTS = 9
LN2 = math.log(2.0)
SCALE = math.sqrt(5.0) / LN2
CURVE = LN2 * LN2 / 3.0
BEND = 3.0 / LN2
LIFT = 3.0 / (LN2 * LN2)
LAST = (((1,), (1,)), ((), ()))


def three(value):
    high = value.astype(BF16).astype(F32)
    rest = value - high
    middle = rest.astype(BF16).astype(F32)
    return high, middle, (rest - middle).astype(BF16).astype(F32)


def two(value):
    high = value.astype(BF16)
    return high, (value - high.astype(F32)).astype(BF16)


def matern(square):
    square = jnp.maximum(square, 1e-30)
    root = square * lax.rsqrt(square)
    return (square + BEND * root + LIFT) * jnp.exp2(-root)


def kernel(
    scales_hbm, noise_hbm, points_hbm, res_hbm, dir_hbm,
    out_ref,
    scales_ref, noise_ref, points_ref, res_ref, dir_ref,
    rows, cols, left, right, dir_row, dir_col, acc_row, acc_col, square, high, low,
    out_row, out_col, in_row, in_col, pair_stat, chip_stat, load_sem,
    row_send, row_near, row_recv, col_send, col_near, col_recv, rs_row_send, rs_row_recv, rs_col_send, rs_col_recv,
    sc_send, sc_recv, sr_send, sr_recv,
):
    me = lax.axis_index("blk")
    down = lax.rem(me // 2, SIDE)
    across = (me // (2 * SIDE)) * 2 + lax.rem(me, 2)

    def device(i, l):
        i, l = lax.rem(i, SIDE), lax.rem(l, SIDE)
        return ((l // 2) * (2 * SIDE) + i * 2 + lax.rem(l, 2),)

    def offset_of(p):
        if isinstance(p, int):
            return PLACES[p]
        offset = PLACES[0]
        for k in range(1, SIDE):
            offset = jnp.where(p == k, PLACES[k], offset)
        return offset

    barrier = pltpu.get_barrier_semaphore()

    def greet(k, _):
        pl.semaphore_signal(barrier, inc=1, device_id=device(down + k, across), device_id_type=MESH)
        pl.semaphore_signal(barrier, inc=1, device_id=device(down, across + k), device_id_type=MESH)
        return 0

    lax.fori_loop(1, SIDE, greet, 0)
    loads = [
        pltpu.make_async_copy(a, b, load_sem.at[k])
        for k, (a, b) in enumerate((
            (points_hbm, points_ref), (scales_hbm, scales_ref), (dir_hbm, dir_ref),
            (noise_hbm, noise_ref), (res_hbm, res_ref)))
    ]
    for load in loads:
        load.start()

    acc_row[...] = jnp.zeros_like(acc_row)
    acc_col[...] = jnp.zeros_like(acc_col)
    for load in loads:
        load.wait()

    line = lax.broadcasted_iota(jnp.int32, (SIDE, 256), 0)
    ratio = jnp.ones((SIDE, 256), F32)
    for f in range(11):
        ratio = jnp.where(line == f, scales_ref[f], ratio)
    cols[OWN, 0:16, :] = dir_ref[...]
    cols[OWN, 16:32, :] = jnp.zeros((16, 256), F32)
    cols[OWN, 16:27, :] = points_ref[...]
    feats = cols[OWN, 16:32, :] * (SCALE / ratio)
    norm = jnp.sum(feats * feats, axis=0, keepdims=True)
    block = jnp.where(line == 11, norm, jnp.where(line == 12, 1.0, feats))
    cols[OWN, 16:32, :] = block
    rows[0, 0:16, :] = dir_ref[...]
    rows[0, 16:32, :] = block

    pl.semaphore_wait(barrier, 2 * (SIDE - 1))

    FEATS, DIRS = pl.ds(16, 16), pl.ds(0, 16)

    def copy_row(s, part):
        return pltpu.make_async_remote_copy(
            src_ref=cols.at[OWN, part], dst_ref=rows.at[s, part], send_sem=row_send,
            recv_sem=(row_near if part is FEATS else row_recv).at[s],
            device_id=device(down, across + SIDE - STEPS[s]), device_id_type=MESH)

    def copy_col(p, part):
        return pltpu.make_async_remote_copy(
            src_ref=cols.at[OWN, part], dst_ref=cols.at[p, part], send_sem=col_send,
            recv_sem=(col_near if part is FEATS else col_recv).at[p],
            device_id=device(down + SIDE - offset_of(p), across), device_id_type=MESH)

    def arrived(ref, sem):
        pltpu.make_async_copy(ref, ref, sem).wait()

    def ship(*lots):
        for make, part, ids in lots:
            for k in ids:
                make(k, part).start()

    ship((copy_row, FEATS, (1, 2, 3)), (copy_col, FEATS, (0, 1, 2, 3)), (copy_row, DIRS, (1, 2, 3)), (copy_row, FEATS, (8,)), (copy_col, FEATS, (4, 5, 6, 7)), (copy_col, DIRS, (0, 1, 2, 3)), (copy_row, FEATS, (6, 7, 4, 5)), (copy_col, FEATS, (8, 9, 10, 11)), (copy_row, DIRS, (8,)), (copy_col, DIRS, (4, 5, 6, 7)),)
    ship((copy_row, DIRS, (6, 7, 4, 5)), (copy_col, DIRS, (8, 9, 10, 11)), (copy_col, FEATS, (12, 13, 14)), (copy_col, DIRS, (12, 13, 14)),)

    def prep_row(s):
        value = rows[s, 16:32, :]
        norm = jnp.sum(jnp.where(line == 11, value, 0.0), axis=0, keepdims=True)
        value = jnp.where(line == 11, 1.0, jnp.where(line == 12, norm, -2.0 * value))
        h, m, l = three(value)
        tall = jnp.concatenate([h, h, m, h, l, m], axis=0)
        left[s] = jnp.transpose(tall).astype(BF16)

    def prep_col(p):
        h, m, l = three(cols[p, 16:32, :])
        right[p] = jnp.concatenate([h, m, h, l, h, m], axis=0).astype(BF16)

    def take_row(s):
        arrived(rows.at[s, FEATS], row_near.at[s])
        prep_row(s)

    def take_col(p):
        arrived(cols.at[p, FEATS], col_near.at[p])
        prep_col(p)

    def take_row_dir(s):
        arrived(rows.at[s, DIRS], row_recv.at[s])
        dir_row[s] = jnp.concatenate(two(rows[s, 0:16, :]), axis=0)

    def split_col_dir(p):
        dir_col[p] = jnp.concatenate(two(cols[p, 0:16, :]), axis=0)

    def take_col_dir(p):
        arrived(cols.at[p, DIRS], col_recv.at[p])
        split_col_dir(p)

    prep_row(0)
    prep_col(OWN)
    own_dir = jnp.concatenate(two(dir_ref[...]), axis=0)
    dir_row[0] = own_dir
    dir_col[OWN] = own_dir

    def places(t):
        near = jnp.where((t < 6) | (t >= 14), 1, 0)
        pair = jnp.where(t < 6, t, jnp.maximum(t - 8, 0))
        quad = jnp.where(t < 10, t - 6, t - 10)
        base = jnp.where(t < 10, 6, 4)
        first = jnp.where((pair >= 2) & (pair <= 5), 8, 0)
        slots, spots = [], []
        for n in range(4):
            slots.append(jnp.where(near == 1, n if n else first, base + n // 2))
            spots.append([jnp.where(near == 1, 2 * pair + j, 4 * quad + n % 2 * 2 + j) for j in range(2)])
        return near, pair, slots, spots

    def dot(a, b):
        return jnp.dot(a, b, preferred_element_type=F32)

    def dot_t(a, b):
        return lax.dot_general(a, b, LAST, preferred_element_type=F32)

    def distance(s, y):
        return dot(left[s], right[y])

    def spread(d, hi, lo, product):
        both, rest = product(d, hi), product(d[0:16], lo)
        return jnp.concatenate([both[0:16] + rest, both[16:32]], axis=0)

    def work(t, apply, entries, distances):
        near, pair, slots, spots = places(t - 2)
        _, _, slots_n, spots_n = places(t)
        one_way = jnp.where((near == 1) & ((pair == 3) | (pair == 7)), 0.0, 1.0).astype(F32)
        for n in range(4):
            mine = None
            for j in range(2):
                k = n * 2 + j
                if apply:
                    hi, lo = high[k], low[k]
                    term = spread(dir_col[spots[n][j]], hi, lo, dot_t)
                    mine = term if mine is None else mine + term
                    term = spread(dir_row[slots[n]], hi, lo, dot)
                    if n == 0 and j == 1:
                        term = term * one_way
                    acc_col[spots[n][j]] += term
                if entries:
                    hi, lo = two(matern(square[k]))
                    high[k] = hi
                    low[k] = lo
                if distances:
                    square[k] = distance(slots_n[n], spots_n[n][j])
            if apply:
                acc_row[slots[n]] += mine

    def give_row(s):
        return pltpu.make_async_remote_copy(
            src_ref=out_row.at[s], dst_ref=in_row.at[s], send_sem=rs_row_send, recv_sem=rs_row_recv,
            device_id=device(down, across + STEPS[s]), device_id_type=MESH)

    def give_col(p):
        return pltpu.make_async_remote_copy(
            src_ref=out_col.at[p], dst_ref=in_col.at[p], send_sem=rs_col_send, recv_sem=rs_col_recv,
            device_id=device(down + offset_of(p), across), device_id_type=MESH)

    def push_row(s):
        out_row[s] = acc_row[s, 0:16, :] + acc_row[s, 16:32, :]
        give_row(s).start()

    def push_col(p):
        out_col[p] = acc_col[p, 0:16, :] + acc_col[p, 16:32, :]
        give_col(p).start()

    for s in (1, 2, 3):
        take_row(s)
    take_col(0)
    take_col(1)
    work(0, False, False, True)
    take_col(2)
    take_col(3)
    work(1, False, True, True)

    def early(t, _):
        @pl.when(t == 2)
        def _():
            take_row(8)
            for s in (1, 2, 3):
                take_row_dir(s)

        @pl.when(t == 4)
        def _():
            take_row_dir(8)

        @pl.when(t == 6)
        def _():
            for s in (4, 5, 6, 7):
                take_row(s)

        for j in range(2):
            arrived(cols.at[2 * t - 4 + j, DIRS], col_recv.at[2 * t - 4 + j])
        arrived(cols.at[2 * t, FEATS], col_near.at[2 * t])

        @pl.when(t <= 6)
        def _():
            arrived(cols.at[2 * t + 1, FEATS], col_near.at[2 * t + 1])

        for j in range(2):
            split_col_dir(2 * t - 4 + j)
            prep_col(2 * t + j)
        work(t, True, True, True)
        return 0

    def late(t, _):
        @pl.when(t == 12)
        def _():
            push_row(7)
            push_row(6)

        @pl.when(t >= 13)
        def _():
            for k in range(4):
                push_col(4 * t - 52 + k)

        work(t, True, True, True)
        return 0

    lax.fori_loop(2, 8, early, 0)
    for s in (4, 5, 6, 7):
        take_row_dir(s)
    for p in (12, 13, 14):
        take_col_dir(p)
    push_row(8)
    lax.fori_loop(8, 16, late, 0)
    push_row(5)
    push_row(4)
    work(16, True, True, False)
    push_col(12)
    push_col(13)
    work(17, True, False, False)
    for s in (3, 2, 1):
        push_row(s)
    push_col(14)
    extra = spread(dir_col[7], *two(matern(distance(0, 7))), dot_t)
    extra = extra + spread(dir_row[8], *two(matern(distance(8, OWN))), dot)
    extra = extra + acc_row[0] + acc_col[OWN]
    own = extra[0:16] + extra[16:32]

    arrived(in_col.at[pl.ds(0, SIDE - 1)], rs_col_recv)
    for p in range(SIDE - 1):
        own = own + in_col[p]
    arrived(in_row.at[pl.ds(1, SLOTS - 1)], rs_row_recv)
    for s in range(1, SLOTS):
        own = own + in_row[s]
    direction = dir_ref[...]
    residual = res_ref[...]
    image = CURVE * own + noise_ref[0] * direction

    def total(value):
        return jnp.sum(value, axis=1, keepdims=True)

    lane = lax.broadcasted_iota(jnp.int32, (16, 128), 1) - lax.broadcasted_iota(jnp.int32, (16, 128), 0)
    stats = jnp.zeros((16, 128), F32)
    for k, value in enumerate((residual * residual, direction * image, residual * image, image * image)):
        stats = jnp.where(lane == 16 * k, total(value), stats)
    stats = jnp.sum(stats, axis=0, keepdims=True)

    core = lax.rem(me, 2)
    pair_stat[0:1, :] = stats
    tell_core = pltpu.make_async_remote_copy(
        src_ref=pair_stat.at[pl.ds(0, 1)], dst_ref=pair_stat.at[pl.ds(8, 1)], send_sem=sc_send, recv_sem=sc_recv,
        device_id=(me + 1 - 2 * core,), device_id_type=MESH)
    tell_core.start()
    zs = [lax.rem(me // 32 + d, 8) * 32 + core for d in range(8)]
    xs = [lax.rem(me // 8 + d, 4) * 8 for d in range(4)]
    ys = [lax.rem(me // 2 + d, 4) * 2 for d in range(4)]
    tell_core.wait_recv()
    chip_stat[0:1, :] = stats + pair_stat[8:9, :]
    for k, (dz, dx, dy) in enumerate(FAR):
        pltpu.make_async_remote_copy(
            src_ref=chip_stat.at[pl.ds(0, 1)], dst_ref=chip_stat.at[pl.ds(k + 1, 1)],
            send_sem=sr_send, recv_sem=sr_recv,
            device_id=(zs[dz] + xs[dx] + ys[dy],), device_id_type=MESH).start()
    others = chip_stat.at[pl.ds(1, len(FAR))]
    arrived(others, sr_recv)
    stats = jnp.sum(chip_stat[...], axis=0, keepdims=True)

    def pick(k):
        return total(jnp.where(lane == 16 * k, stats, 0.0))

    rr, pap, cross, squared = pick(0), pick(1), pick(2), pick(3)
    alpha = rr / pap
    rr_next = jnp.maximum(rr - alpha * (2.0 * cross - alpha * squared), 0.0)
    out_ref[0:16, :] = image
    out_ref[16:32, :] = jnp.broadcast_to(alpha, (16, 256))
    out_ref[32:48, :] = jnp.broadcast_to(rr_next / rr, (16, 256))

    arrived(rows.at[pl.ds(1, SLOTS - 1)], row_send)
    arrived(cols.at[pl.ds(0, SIDE - 1)], col_send)
    arrived(out_row.at[pl.ds(1, SLOTS - 1)], rs_row_send)
    arrived(out_col.at[pl.ds(0, SIDE - 1)], rs_col_send)
    tell_core.wait_send()
    arrived(others, sr_send)


def on_device(points, lengthscales, noise, solution, residual, direction):
    vmem = pl.BlockSpec(memory_space=pltpu.VMEM)
    out = jax.ShapeDtypeStruct((16, 256), F32)
    dma = pltpu.SemaphoreType.DMA
    packed = pl.pallas_call(
        kernel,
        out_shape=jax.ShapeDtypeStruct((48, 256), F32),
        in_specs=[pl.BlockSpec(memory_space=pltpu.HBM)] * 5,
        out_specs=vmem,
        scratch_shapes=[
            pltpu.SMEM((11,), F32), pltpu.SMEM((1,), F32), pltpu.VMEM((11, 256), F32),
            pltpu.VMEM((16, 256), F32), pltpu.VMEM((16, 256), F32),
            pltpu.VMEM((SLOTS, 32, 256), F32), pltpu.VMEM((SIDE, 32, 256), F32),
            pltpu.VMEM((SLOTS, 256, 96), BF16), pltpu.VMEM((SIDE, 96, 256), BF16),
            pltpu.VMEM((SLOTS, 32, 256), BF16), pltpu.VMEM((SIDE, 32, 256), BF16),
            pltpu.VMEM((SLOTS, 32, 256), F32), pltpu.VMEM((SIDE, 32, 256), F32),
            pltpu.VMEM((8, 256, 256), F32), pltpu.VMEM((8, 256, 256), BF16), pltpu.VMEM((8, 256, 256), BF16),
            pltpu.VMEM((SLOTS, 16, 256), F32), pltpu.VMEM((SIDE, 16, 256), F32),
            pltpu.VMEM((SLOTS, 16, 256), F32), pltpu.VMEM((SIDE, 16, 256), F32),
            pltpu.VMEM((16, 128), F32), pltpu.VMEM((128, 128), F32), dma((5,)),
            dma, dma((SLOTS,)), dma((SLOTS,)), dma, dma((SIDE,)), dma((SIDE,)),
            dma, dma, dma, dma, dma, dma, dma, dma,
        ],
        compiler_params=pltpu.CompilerParams(
            collective_id=0, has_side_effects=True, vmem_limit_bytes=60 * 2**20),
    )(lengthscales, noise, points, residual, direction)
    image, alpha, beta = packed[0:16], packed[16:32], packed[32:48]
    residual_next = residual - alpha * image
    return solution + alpha * direction, residual_next, residual_next + beta * direction


def solution(mesh):
    placed = (P(None, "blk"), P(), P(), P(None, "blk"), P(None, "blk"), P(None, "blk"))
    return jax.shard_map(
        on_device,
        mesh=mesh,
        in_specs=placed,
        out_specs=(P(None, "blk"), P(None, "blk"), P(None, "blk")),
        check_vma=False,
    )
```
